256 devices in a mesh: seq: 16 (over y_lo, x, core), head: 16 (over y_hi, z).
Axes of the slice: x: 4, y: 4 (y_hi: 2, y_lo: 2; y = y_hi * 2 + y_lo), z: 8, core: 2. Of those that a mesh axis runs over, the one named last changes fastest.
Arguments:
- queries: bfloat16 [2048, 8192], P('seq', 'head'), may hold values from -16 to 16
- cache_keys: bfloat16 [32768, 1024], P('seq'), may hold values from -16 to 16
- cache_values: bfloat16 [32768, 1024], P('seq'), may hold values from -6 to 6
- new_keys: bfloat16 [2048, 1024], P('seq'), may hold values from -6 to 6
- new_values: bfloat16 [2048, 1024], P('seq'), may hold values from -6 to 6
- out_weight: bfloat16 [8192, 8192], P('seq', 'head'), may hold values from -0.0625 to 0.0625
Outputs:
- mixed: bfloat16 [2048, 8192], P('seq', 'head')
The draws below stay inside these ranges and needn't reach their ends.
All inputs are finite; a program needn't handle non-finite values.
Results may differ from the reference program's by a relative error of at most 0.028.
Values may be sent and summed in bfloat16 or wider, within the bound.
A program may use at most 128 MiB of HBM per device.

```python
import jax
import jax.numpy as jnp
from jax import lax

D = 8192
HQ = 64
KV = 8
HD = 128
PREFIX = 32768
STRETCH = 2048


def draw_queries(key, part):
    key = jax.random.fold_in(key, 11)
    values_drawn = jnp.clip(jax.random.normal(key, (STRETCH, HQ, HD), jnp.float32), -6.0, 6.0)
    return values_drawn.reshape(STRETCH, HQ * HD).astype(jnp.bfloat16)


def draw_cache_keys(key, part):
    key = jax.random.fold_in(key, 23)
    values_drawn = jnp.clip(jax.random.normal(key, (PREFIX, KV, HD), jnp.float32), -6.0, 6.0)
    return values_drawn.reshape(PREFIX, KV * HD).astype(jnp.bfloat16)


def block_scale(key, shape, shards, smallest, largest):
    gain, own = 1.0, jax.random.fold_in(key, 6)
    for position, parts in shards:
        draws = jnp.exp(jax.random.uniform(jax.random.fold_in(own, position), (parts,), jnp.float32, smallest / len(shards), largest / len(shards)))
        gain = gain * jnp.repeat(draws, shape[position] // parts).reshape([-1 if axis == position else 1 for axis in range(len(shape))])
    return gain


def bell_draw(key, shape, deviation, bound, split=(), kind=jnp.bfloat16):
    values = jax.random.normal(key, shape, jnp.float32) * deviation
    if len(split) > 0:
        values = block_scale(key, shape, split, -0.22, 0.18) * values
    return jnp.clip(values, min=-bound, max=bound).astype(kind)


def setup_inputs(seed: int = 0) -> dict:
    streams_of = jax.random.split(jax.random.key(seed), 7)
    return {
        "queries": draw_queries(jax.random.fold_in(streams_of[6], 71), 0),
        "cache_keys": draw_cache_keys(jax.random.fold_in(streams_of[6], 71), 0),
        "cache_values": bell_draw(streams_of[2], (PREFIX, KV * HD), 1.0, 6.0, ((0, 16),)),
        "new_keys": bell_draw(streams_of[3], (STRETCH, KV * HD), 1.0, 6.0, ((0, 16),)),
        "new_values": bell_draw(streams_of[4], (STRETCH, KV * HD), 1.0, 6.0, ((0, 16),)),
        "out_weight": bell_draw(streams_of[5], (HQ * HD, D), (HQ * HD) ** -0.5, 0.0625, ((0, 16), (1, 16))),
    }


def reference(queries, cache_keys, cache_values, new_keys, new_values, out_weight):
    all_keys = jnp.concatenate([cache_keys, new_keys], 0)
    all_values = jnp.concatenate([cache_values, new_values], 0)
    query_pos = jnp.arange(STRETCH, dtype=jnp.int32)
    key_pos = jnp.concatenate([jnp.full((PREFIX,), -1, jnp.int32), jnp.arange(STRETCH, dtype=jnp.int32)])
    visible = key_pos[None, :] <= query_pos[:, None]
    group_size = HQ // KV

    def one_head(head_id):
        query_cols = lax.dynamic_slice_in_dim(queries, head_id * HD, HD, 1)
        kv_head = head_id // group_size
        key_cols = lax.dynamic_slice_in_dim(all_keys, kv_head * HD, HD, 1)
        value_cols = lax.dynamic_slice_in_dim(all_values, kv_head * HD, HD, 1)
        scores = jnp.dot(query_cols, key_cols.T, preferred_element_type=jnp.float32) * (HD ** -0.5)
        scores = jnp.where(visible, scores, -1e30)
        top_score = jnp.max(scores, axis=1, keepdims=True)
        weights = jnp.where(visible, jnp.exp(scores - top_score), 0.0)
        weight_sum = jnp.sum(weights, axis=1, keepdims=True)
        summed = jnp.dot(weights.astype(jnp.bfloat16), value_cols, preferred_element_type=jnp.float32)
        return (summed / weight_sum).astype(jnp.bfloat16)

    per_head = lax.map(one_head, jnp.arange(HQ, dtype=jnp.int32))
    attended = jnp.transpose(per_head, (1, 0, 2)).reshape(STRETCH, HQ * HD)
    return jnp.dot(attended, out_weight, preferred_element_type=jnp.float32).astype(jnp.bfloat16)
```

```python
import functools

import jax
import jax.numpy as jnp
import numpy as np
from jax import lax
from jax.experimental import pallas as pl
from jax.experimental.pallas import tpu as pltpu
from jax.sharding import PartitionSpec as P

HD = 128
G = 4
COLS = G * 128
SHARD = 2048
CACHED = 2 * SHARD
KEYS = CACHED + 256
TK = 256
VR = 144
SCALE = float(HD**-0.5 * np.log2(np.e))
MESH = pl.DeviceIdType.MESH
F32, BF16 = jnp.float32, jnp.bfloat16


def kernel(
    q_ref, ck_ref, cv_ref, nk_ref, nv_ref, w_ref, out_ref,
    k2, vraw, vt, sbuf, qbuf, qt, osend, ssend, obuf, stbuf, abuf, wbuf, acc, csend, cbuf,
    loc_sem, kv_send, kv_recv, q_send, q_recv, w_send, w_recv, wf_send,
    o_send, o_recv, st_send, st_recv, a_send, a_recv, c_send, c_recv,
):
    s = lax.axis_index("seq")
    h = lax.axis_index("head")
    yl, x, c = s // 8, (s // 2) % 4, s % 2
    yh, z = h // 8, h % 8
    me_block = yl * 4 + x
    partner = (s + 1 - 2 * c, h)
    self_combine = yl == yh

    def seq_of(a, b):
        return a * 8 + b * 2 + c

    def item(i):
        step = i // 2
        gray = jnp.where(step == 2, 3, jnp.where(step == 3, 2, step))
        return (yl + i) % 2, (x + gray) % 4

    def remote(src, dst, ssem, rsem, dev):
        return pltpu.make_async_remote_copy(
            src_ref=src, dst_ref=dst, send_sem=ssem, recv_sem=rsem, device_id=dev, device_id_type=MESH
        )

    def arrived(ref, sem):
        pltpu.make_async_copy(ref, ref, sem).wait()

    kv_col = pl.ds(pl.multiple_of((h // 2) * HD, HD), HD)

    def cached_rows(core):
        return pl.ds(pl.multiple_of(core * SHARD, SHARD), SHARD)

    def new_rows(core):
        return pl.ds(pl.multiple_of(CACHED + core * 128, 128), 128)

    def kv_parts(core):
        return [
            (ck_ref.at[:, kv_col], k2.at[cached_rows(core), pl.ds(0, HD)]),
            (ck_ref.at[:, kv_col], k2.at[cached_rows(core), pl.ds(HD, HD)]),
            (nk_ref.at[:, kv_col], k2.at[new_rows(core), pl.ds(0, HD)]),
            (nk_ref.at[:, kv_col], k2.at[new_rows(core), pl.ds(HD, HD)]),
            (cv_ref.at[:, kv_col], vraw.at[cached_rows(core), :]),
            (nv_ref.at[:, kv_col], vraw.at[new_rows(core), :]),
        ]

    local = [
        pltpu.make_async_copy(src, dst, loc_sem.at[n]) for n, (src, dst) in enumerate(kv_parts(c))
    ]
    local.append(pltpu.make_async_copy(w_ref, wbuf.at[x * 2 + c], loc_sem.at[6]))
    local.append(pltpu.make_async_copy(q_ref, qbuf.at[me_block], loc_sem.at[7]))
    for copy in local:
        copy.start()

    barrier = pltpu.get_barrier_semaphore()

    def greet(dev):
        pl.semaphore_signal(barrier, inc=1, device_id=dev, device_id_type=MESH)

    for i in range(1, 8):
        b0, b1 = item(i)
        greet((seq_of(b0, b1), h))
    greet(partner)
    greet((s, yh * 8 + (z + 1) % 8))
    greet((s, yh * 8 + (z + 7) % 8))
    greet((s, (1 - yh) * 8 + z))
    for i in range(8):
        b0, b1 = item(i)
        if i == 0:
            @pl.when(jnp.logical_not(self_combine))
            def _():
                greet((seq_of(b0, b1), yl * 8 + z))
        else:
            greet((seq_of(b0, b1), yl * 8 + z))
    pl.semaphore_wait(barrier, jnp.where(self_combine, 18, 19))

    kv_out = [
        remote(src, dst, kv_send.at[n], kv_recv.at[n], partner)
        for n, (src, dst) in enumerate(kv_parts(c))
    ]
    for copy in kv_out:
        copy.start()

    def q_copy(i):
        b0, b1 = item(i)
        return remote(q_ref, qbuf.at[me_block], q_send.at[i], q_recv.at[me_block], (seq_of(b0, b1), h))

    for i in range(1, 8):
        q_copy(i).start()

    my_w = x * 2 + c

    def w_copy(d):
        return remote(w_ref, wbuf.at[my_w], w_send.at[d], w_recv.at[my_w], (seq_of(yl, (x + d) % 4), h))

    def w_forward(d):
        slot = ((x + 4 - d) % 4) * 2 + c
        return remote(wbuf.at[slot], wbuf.at[slot], wf_send.at[d], w_recv.at[slot], partner)

    for d in (1, 3, 2):
        w_copy(d).start()

    def flip(rows):
        vt[pl.ds(0, HD), rows] = vraw[rows, :].T

    vt[pl.ds(HD, VR - HD), :] = jnp.ones((VR - HD, KEYS), BF16)
    for copy in local:
        copy.wait()

    def flip_cached(core):
        def one(t, unused):
            flip(pl.ds(pl.multiple_of(core * SHARD + t * TK, TK), TK))
            return unused

        lax.fori_loop(0, SHARD // TK, one, 0)

    w_forward(0).start()
    flip_cached(c)
    for copy in kv_out:
        copy.wait_recv()
    flip_cached(1 - c)
    flip(pl.ds(CACHED, 256))

    def o_dest(i):
        b0, b1 = item(i)
        return (seq_of(yh, b1), b0 * 8 + z)

    def o_is_self(i):
        b0, b1 = item(i)
        return jnp.logical_and(self_combine, jnp.logical_and(b0 == yh, b1 == x))

    def o_copies(i):
        return (
            remote(osend.at[i], obuf.at[me_block], o_send.at[i], o_recv.at[me_block], o_dest(i)),
            remote(ssend.at[i], stbuf.at[me_block], st_send.at[i], st_recv.at[me_block], o_dest(i)),
        )

    def o_local(i):
        return (
            pltpu.make_async_copy(osend.at[i], obuf.at[me_block], o_recv.at[me_block]),
            pltpu.make_async_copy(ssend.at[i], stbuf.at[me_block], st_recv.at[me_block]),
        )

    def one_item(i, unused):
        b0, b1 = item(i)
        block = b0 * 4 + b1

        @pl.when(i > 0)
        def _():
            arrived(qbuf.at[block], q_recv.at[block])

        q = qbuf[block]
        tall = jnp.concatenate([q[:, g * HD : (g + 1) * HD] for g in range(G)], axis=0)
        wide = tall.astype(F32).T * SCALE
        high = wide.astype(BF16)
        qt[pl.ds(0, HD), :] = high
        qt[pl.ds(HD, HD), :] = (wide - high.astype(F32)).astype(BF16)

        top = jnp.full((8, COLS), -1e30, F32)
        for t in range(KEYS // TK):
            scores = jnp.dot(k2[pl.ds(t * TK, TK), :], qt[...], preferred_element_type=F32)
            if t == CACHED // TK:
                key_pos = (yl * 8 + x * 2) * 128 + lax.broadcasted_iota(jnp.int32, (TK, COLS), 0)
                row = lax.broadcasted_iota(jnp.int32, (TK, COLS), 1) % 128
                visible = key_pos <= seq_of(b0, b1) * 128 + row
                scores = jnp.where(visible, scores, -1e30)
            sbuf[pl.ds(t * TK, TK), :] = scores
            top = jnp.maximum(top, jnp.max(scores.reshape(TK // 8, 8, COLS), axis=0))
        top = jnp.max(top, axis=0, keepdims=True)
        summed = jnp.zeros((VR, COLS), F32)
        for t in range(KEYS // TK):
            weights = jnp.exp2(sbuf[pl.ds(t * TK, TK), :] - top).astype(BF16)
            summed = summed + jnp.dot(vt[:, pl.ds(t * TK, TK)], weights, preferred_element_type=F32)
        total = summed[HD : HD + 1]
        osend[i] = (summed[:HD] / total).astype(BF16)
        ssend[i] = jnp.concatenate([top, total, jnp.zeros((6, COLS), F32)], axis=0)

        is_self = o_is_self(i)

        @pl.when(is_self)
        def _():
            for copy in o_local(i):
                copy.start()

        @pl.when(jnp.logical_not(is_self))
        def _():
            for copy in o_copies(i):
                copy.start()

        return unused

    lax.fori_loop(0, 8, one_item, 0)

    for d in (1, 3, 2):
        slot = ((x + 4 - d) % 4) * 2 + c
        arrived(wbuf.at[slot], w_recv.at[slot])
        w_forward(d).start()

    for j in range(8):
        arrived(obuf.at[j], o_recv.at[j])
        arrived(stbuf.at[j], st_recv.at[j])
    tops = [stbuf[j, 0:1, :] for j in range(8)]
    top = functools.reduce(jnp.maximum, tops)
    parts = [stbuf[j, 1:2, :] * jnp.exp2(tops[j] - top) for j in range(8)]
    total = functools.reduce(jnp.add, parts)
    joined = jnp.zeros((HD, COLS), F32)
    for j in range(8):
        joined = joined + obuf[j].astype(F32) * (parts[j] / total)
    mine = yh * 8 + z
    for g in range(G):
        abuf[mine, :, pl.ds(g * HD, HD)] = joined[:, g * HD : (g + 1) * HD].T.astype(BF16)

    right = (s, yh * 8 + (z + 1) % 8)
    left = (s, yh * 8 + (z + 7) % 8)
    across = (s, (1 - yh) * 8 + z)

    def slot_of(plane, zz):
        return plane * 8 + (zz + 8) % 8

    def hand(slot, n, dev):
        return remote(abuf.at[slot], abuf.at[slot], a_send.at[n], a_recv.at[slot], dev)

    sent = []

    def send(slot, dev):
        copy = hand(slot, len(sent), dev)
        copy.start()
        sent.append(copy)

    def take(slot):
        arrived(abuf.at[slot], a_recv.at[slot])

    acc[...] = jnp.zeros_like(acc)

    def multiply(plane, zz):
        zz = (zz + 8) % 8

        for n in range(2):
            cols = pl.ds(n * 256, 256)
            acc[plane, :, cols] += jnp.dot(
                abuf[plane * 8 + zz], wbuf[zz, :, cols], preferred_element_type=F32
            )

    own, other = yh, 1 - yh
    send(mine, right)
    send(mine, left)
    send(mine, across)
    for d in range(4):
        slot = ((x + 4 - d) % 4) * 2 + 1 - c
        arrived(wbuf.at[slot], w_recv.at[slot])
    multiply(own, z)
    take(slot_of(other, z))
    send(slot_of(other, z), right)
    send(slot_of(other, z), left)
    multiply(other, z)
    for t in range(1, 5):
        take(slot_of(own, z - t))
        if t < 4:
            send(slot_of(own, z - t), right)
        if t < 4:
            take(slot_of(own, z + t))
            if t < 3:
                send(slot_of(own, z + t), left)
            take(slot_of(other, z - t))
            if t < 3:
                send(slot_of(other, z - t), right)
        take(slot_of(other, z + t))
        if t < 4:
            send(slot_of(other, z + t), left)
        multiply(own, z - t)
        if t < 4:
            multiply(own, z + t)
            multiply(other, z - t)
        multiply(other, z + t)

    csend[...] = acc[1 - yl].astype(BF16)
    swap = remote(csend, cbuf, c_send, c_recv, (seq_of(1 - yl, x), h))
    swap.start()
    swap.wait()
    out_ref[...] = (acc[yl] + cbuf[...].astype(F32)).astype(BF16)

    for copy in sent:
        copy.wait_send()
    for copy in kv_out:
        copy.wait_send()
    for i in range(1, 8):
        q_copy(i).wait_send()
    for d in (1, 2, 3):
        w_copy(d).wait_send()
    for d in range(4):
        w_forward(d).wait_send()

    def drain(i, unused):
        @pl.when(jnp.logical_not(o_is_self(i)))
        def _():
            for copy in o_copies(i):
                copy.wait_send()

        return unused

    lax.fori_loop(0, 8, drain, 0)


def local(queries, cache_keys, cache_values, new_keys, new_values, out_weight):
    dma = pltpu.SemaphoreType.DMA
    hbm = pl.BlockSpec(memory_space=pl.ANY)
    vmem = pl.BlockSpec(memory_space=pltpu.VMEM)
    return pl.pallas_call(
        kernel,
        out_shape=jax.ShapeDtypeStruct((128, 512), BF16),
        in_specs=[vmem, hbm, hbm, hbm, hbm, hbm],
        out_specs=vmem,
        scratch_shapes=[
            pltpu.VMEM((KEYS, 2 * HD), BF16),
            pltpu.VMEM((KEYS, HD), BF16),
            pltpu.VMEM((VR, KEYS), BF16),
            pltpu.VMEM((KEYS, COLS), F32),
            pltpu.VMEM((8, 128, COLS), BF16),
            pltpu.VMEM((2 * HD, COLS), BF16),
            pltpu.VMEM((8, HD, COLS), BF16),
            pltpu.VMEM((8, 8, COLS), F32),
            pltpu.VMEM((8, HD, COLS), BF16),
            pltpu.VMEM((8, 8, COLS), F32),
            pltpu.VMEM((16, 128, COLS), BF16),
            pltpu.VMEM((8, 512, 512), BF16),
            pltpu.VMEM((2, 128, 512), F32),
            pltpu.VMEM((128, 512), BF16),
            pltpu.VMEM((128, 512), BF16),
            dma((8,)), dma((6,)), dma((6,)), dma((8,)), dma((8,)),
            dma((4,)), dma((8,)), dma((4,)),
            dma((8,)), dma((8,)), dma((8,)), dma((8,)),
            dma((15,)), dma((16,)), dma, dma,
        ],
        compiler_params=pltpu.CompilerParams(
            collective_id=0, has_side_effects=True, vmem_limit_bytes=48 * 2**20
        ),
        cost_estimate=pl.CostEstimate(
            flops=11_000_000_000, bytes_accessed=4_000_000, transcendentals=18_000_000
        ),
    )(queries, cache_keys, cache_values, new_keys, new_values, out_weight)


def solution(mesh):
    placed = (
        P("seq", "head"),
        P("seq", None),
        P("seq", None),
        P("seq", None),
        P("seq", None),
        P("seq", "head"),
    )
    return jax.shard_map(
        local, mesh=mesh, in_specs=placed, out_specs=P("seq", "head"), check_vma=False
    )
```

```python
import functools

import jax
import jax.numpy as jnp
import numpy as np
from jax import lax
from jax.experimental import pallas as pl
from jax.experimental.pallas import tpu as pltpu
from jax.sharding import PartitionSpec as P

HD = 128
G = 4
CH = 4
RG = 128 // CH
COLS = 512
HALF = COLS // 2
SHARD = 2048
CACHED = 2 * SHARD
KEYS = CACHED + 256
TK = 256
VR = 144
SCALE = float(HD**-0.5 * np.log2(np.e))
MESH = pl.DeviceIdType.MESH
F32, BF16 = jnp.float32, jnp.bfloat16


def pieces(row):
    a = row.astype(BF16).astype(F32)
    b = (row - a).astype(BF16).astype(F32)
    return [a, b, row - a - b]


def message(result, top, total):
    zeros = jnp.zeros((10, result.shape[1]), F32)
    tail = jnp.concatenate(pieces(top) + pieces(total) + [zeros], axis=0)
    return jnp.concatenate([result.astype(BF16), tail.astype(BF16)], axis=0)


def merge(messages):
    tops, totals = [], []
    for one in messages:
        tail = one[HD:].astype(F32)
        tops.append(tail[0:1] + tail[1:2] + tail[2:3])
        totals.append(tail[3:4] + tail[4:5] + tail[5:6])
    top = functools.reduce(jnp.maximum, tops)
    parts = [b * jnp.exp2(a - top) for a, b in zip(tops, totals)]
    total = functools.reduce(jnp.add, parts)
    result = functools.reduce(
        jnp.add, [one[:HD].astype(F32) * (part / total) for one, part in zip(messages, parts)]
    )
    return result, top, total


def kernel(
    q_ref, ck_ref, cv_ref, nk_ref, nv_ref, w_ref, out_ref,
    k2, vraw, vt, sbuf, qbuf, qt, keep, ysend, yrecv, xsend, xbuf, amine, abuf, wbuf, acc, csend, cbuf,
    loc_sem, kv_send, kv_recv, q_send, q_recv, w_send, w_recv, wf_send,
    y_send, y_recv, x_send, x_recv, m_send, m_recv, z_send, z_recv, h_recv, c_send, c_recv,
):
    s = lax.axis_index("seq")
    h = lax.axis_index("head")
    yl, x, c = s // 8, (s // 2) % 4, s % 2
    yh, z = h // 8, h % 8
    me_block = yl * 4 + x
    partner = (s + 1 - 2 * c, h)

    def seq_of(a, b):
        return a * 8 + b * 2 + c

    y_mate = (seq_of(1 - yl, x), h)

    def remote(src, dst, ssem, rsem, dev):
        return pltpu.make_async_remote_copy(
            src_ref=src, dst_ref=dst, send_sem=ssem, recv_sem=rsem, device_id=dev, device_id_type=MESH
        )

    def arrived(ref, sem):
        pltpu.make_async_copy(ref, ref, sem).wait()

    def when(condition):
        return pl.when(condition)

    kv_col = pl.ds(pl.multiple_of((h // 2) * HD, HD), HD)

    def cached_rows(core):
        return pl.ds(pl.multiple_of(core * SHARD, SHARD), SHARD)

    def new_rows(core):
        return pl.ds(pl.multiple_of(CACHED + core * 128, 128), 128)

    def kv_parts(core):
        return [
            (ck_ref.at[:, kv_col], k2.at[cached_rows(core), pl.ds(0, HD)]),
            (ck_ref.at[:, kv_col], k2.at[cached_rows(core), pl.ds(HD, HD)]),
            (nk_ref.at[:, kv_col], k2.at[new_rows(core), pl.ds(0, HD)]),
            (nk_ref.at[:, kv_col], k2.at[new_rows(core), pl.ds(HD, HD)]),
            (cv_ref.at[:, kv_col], vraw.at[cached_rows(core), :]),
            (nv_ref.at[:, kv_col], vraw.at[new_rows(core), :]),
        ]

    local = [
        pltpu.make_async_copy(src, dst, loc_sem.at[n]) for n, (src, dst) in enumerate(kv_parts(c))
    ]
    local.append(pltpu.make_async_copy(w_ref, wbuf.at[x * 2 + c], loc_sem.at[6]))
    local.append(pltpu.make_async_copy(q_ref, qbuf.at[me_block], loc_sem.at[7]))
    for copy in local:
        copy.start()

    barrier = pltpu.get_barrier_semaphore()

    def greet(dev):
        pl.semaphore_signal(barrier, inc=1, device_id=dev, device_id_type=MESH)

    def peer(n):
        return (seq_of((yl + n % 2) % 2, (x + n // 2) % 4), h)

    for n in range(1, 8):
        greet(peer(n))
    right = (s, yh * 8 + (z + 1) % 8)
    left = (s, yh * 8 + (z + 7) % 8)
    greet(partner)
    greet(right)
    greet(left)
    for a in range(2):
        @when(jnp.logical_or(yl != yh, yl != a))
        def _():
            greet((seq_of(a, x), yl * 8 + z))

    pl.semaphore_wait(barrier, jnp.where(yl == yh, 11, 12))

    kv_out = [
        remote(src, dst, kv_send.at[n], kv_recv.at[n], partner)
        for n, (src, dst) in enumerate(kv_parts(c))
    ]

    def q_copy(g, n):
        rows = pl.ds(pl.multiple_of(g * RG, RG), RG)
        return remote(
            q_ref.at[rows], qbuf.at[me_block, rows], q_send.at[g, n], q_recv.at[g, me_block], peer(n)
        )

    def q_start(g):
        for n in (1, 2, 6, 3, 7, 4, 5):
            q_copy(g, n).start()

    q_start(0)
    for copy in kv_out:
        copy.start()

    my_w = x * 2 + c

    def w_copy(d):
        return remote(w_ref, wbuf.at[my_w], w_send.at[d], w_recv.at[my_w], (seq_of(yl, (x + d) % 4), h))

    def w_slot(d):
        return ((x + 4 - d) % 4) * 2 + c

    def w_forward(d):
        slot = w_slot(d)
        return remote(wbuf.at[slot], wbuf.at[slot], wf_send.at[d], w_recv.at[slot], partner)

    def w_hand_on(d):
        arrived(wbuf.at[w_slot(d)], w_recv.at[w_slot(d)])
        w_forward(d).start()

    def flip(rows):
        vt[pl.ds(0, HD), rows] = vraw[rows, :].T

    def flip_cached(core):
        def one(t, unused):
            flip(pl.ds(pl.multiple_of(core * SHARD + t * TK, TK), TK))
            return unused

        lax.fori_loop(0, SHARD // TK, one, 0)

    vt[pl.ds(HD, VR - HD), :] = jnp.ones((VR - HD, KEYS), BF16)
    for copy in local:
        copy.wait()
    flip_cached(c)

    def reduce_y_start(i):
        return remote(ysend.at[i], yrecv.at[i], y_send.at[i], y_recv.at[i], y_mate)

    def x_dest(i, k):
        return (x + 2 * (i % 2) + k) % 4

    def x_copy(i, k):
        return remote(
            xsend.at[i, k], xbuf.at[i // 2, x], x_send.at[i, k], x_recv.at[i // 2, x],
            (seq_of(yl, x_dest(i, k)), h),
        )

    def stage_x(i):
        arrived(yrecv.at[i], y_recv.at[i])
        merged = message(*merge([keep[i % 2], yrecv[i]]))
        for k in range(2):
            xsend[i, k] = merged[:, k * HD : (k + 1) * HD]
        x_copy(i, 1).start()

        @when(i % 2 == 0)
        def _():
            pltpu.make_async_copy(xsend.at[i, 0], xbuf.at[i // 2, x], x_recv.at[i // 2, x]).start()

        @when(i % 2 == 1)
        def _():
            x_copy(i, 0).start()

    def m_copy(g, a):
        return remote(
            amine.at[g], abuf.at[z, g, yl], m_send.at[g, a], m_recv.at[g, yl], (seq_of(yh, x), a * 8 + z)
        )

    def m_is_self(a):
        return jnp.logical_and(yl == yh, yh == a)

    def stage_m(g):
        for j in range(4):
            arrived(xbuf.at[g, j], x_recv.at[g, j])
        result, _, _ = merge([xbuf[g, j] for j in range(4)])
        turned = result.T.astype(BF16)
        for n in range(G):
            amine[g, :, pl.ds(n * HD, HD)] = turned[n * RG : (n + 1) * RG]
        for a in range(2):
            @when(m_is_self(a))
            def _():
                pltpu.make_async_copy(amine.at[g], abuf.at[z, g, yl], m_recv.at[g, yl]).start()

            @when(jnp.logical_not(m_is_self(a)))
            def _():
                m_copy(g, a).start()

    def zz(d):
        return (z + 8 + d) % 8

    def z_copy(g, t, way):
        slot = zz(-t) if way == 0 else zz(t)
        dev = right if way == 0 else left
        if t < 3:
            ref, sem = abuf.at[slot, g], z_recv.at[g, slot]
        else:
            ref, sem = abuf.at[slot, g, way], h_recv.at[g, way]
        return remote(ref, ref, z_send.at[g, t, way], sem, dev)

    def z_wait(g, t):
        if t == 0:
            for a in range(2):
                arrived(abuf.at[z, g, a], m_recv.at[g, a])
        elif t < 4:
            for d in (-t, t):
                arrived(abuf.at[zz(d), g], z_recv.at[g, zz(d)])
        else:
            for a in range(2):
                arrived(abuf.at[zz(4), g, a], h_recv.at[g, a])

    def stage_z(g, t):
        z_wait(g, t)
        if t < 4:
            for way in range(2):
                z_copy(g, t, way).start()

    def one_item(i, unused):
        g, sub = i // 2, i % 2
        places = [((yl + dy) % 2, (x + 2 * sub + k) % 4) for dy in range(2) for k in range(2)]

        @when(jnp.logical_and(sub == 0, g < CH - 1))
        def _():
            q_start(g + 1)

        rows = pl.ds(pl.multiple_of(g * RG, RG), RG)
        for n, (a, b) in enumerate(places):
            block = a * 4 + b
            if n == 0:
                @when(sub > 0)
                def _():
                    arrived(qbuf.at[block, rows], q_recv.at[g, block])
            else:
                arrived(qbuf.at[block, rows], q_recv.at[g, block])
        tall = jnp.concatenate(
            [qbuf[a * 4 + b, rows, pl.ds(n * HD, HD)] for a, b in places for n in range(G)], axis=0
        )
        wide = tall.astype(F32).T * SCALE
        high = wide.astype(BF16)
        qt[pl.ds(0, HD), :] = high
        qt[pl.ds(HD, HD), :] = (wide - high.astype(F32)).astype(BF16)

        def score(rows):
            return jnp.dot(k2[rows, :], qt[...], preferred_element_type=F32)

        def highest(top, scores):
            return jnp.maximum(top, jnp.max(scores.reshape(TK // 8, 8, COLS), axis=0))

        top = jnp.full((8, COLS), -1e30, F32)
        for core in (c, 1 - c):
            for t in range(SHARD // TK):
                rows = pl.ds(pl.multiple_of(core * SHARD + t * TK, TK), TK)
                scores = score(rows)
                sbuf[rows, :] = scores
                top = highest(top, scores)
            if core is c:
                @when(i == 0)
                def _():
                    for copy in kv_out[:4]:
                        copy.wait_recv()

        col = lax.broadcasted_iota(jnp.int32, (1, COLS), 1)
        base = jnp.zeros((1, COLS), jnp.int32)
        for n, (a, b) in enumerate(places):
            base = jnp.where(col // HD == n, seq_of(a, b) * 128, base)
        query_pos = base + g * RG + col % RG
        rows = pl.ds(CACHED, TK)
        key_pos = (yl * 8 + x * 2) * 128 + lax.broadcasted_iota(jnp.int32, (TK, COLS), 0)
        scores = jnp.where(key_pos <= query_pos, score(rows), -1e30)
        sbuf[rows, :] = scores
        top = jnp.max(highest(top, scores), axis=0, keepdims=True)

        @when(i == 0)
        def _():
            for copy in kv_out[4:]:
                copy.wait_recv()
            flip_cached(1 - c)
            flip(pl.ds(CACHED, 256))

        @when(i > 0)
        def _():
            stage_x(i - 1)

        @when(jnp.logical_and(sub == 1, i >= 3))
        def _():
            stage_z((i - 3) // 2, 0)

        @when(jnp.logical_and(sub == 0, i >= 4))
        def _():
            stage_z((i - 4) // 2, 2)

        summed = jnp.zeros((VR, COLS), F32)
        for t in range(KEYS // TK):
            weights = jnp.exp2(sbuf[pl.ds(t * TK, TK), :] - top).astype(BF16)
            summed = summed + jnp.dot(vt[:, pl.ds(t * TK, TK)], weights, preferred_element_type=F32)
        total = summed[HD : HD + 1]
        packed = message(summed[:HD] / total, top, total)
        keep[i % 2] = packed[:, :HALF]
        ysend[i] = packed[:, HALF:]
        reduce_y_start(i).start()

        @when(jnp.logical_and(sub == 0, i >= 2))
        def _():
            stage_m((i - 2) // 2)

        @when(jnp.logical_and(sub == 1, i >= 3))
        def _():
            stage_z((i - 3) // 2, 1)

        @when(jnp.logical_and(sub == 0, i >= 4))
        def _():
            stage_z((i - 4) // 2, 3)

        @when(i == 0)
        def _():
            w_forward(0).start()
            w_copy(1).start()

        @when(i == 1)
        def _():
            w_copy(3).start()

        @when(i == 2)
        def _():
            w_copy(2).start()

        @when(i == 5)
        def _():
            w_hand_on(1)

        @when(i == 6)
        def _():
            w_hand_on(3)

        return unused

    lax.fori_loop(0, 2 * CH, one_item, 0)

    stage_x(2 * CH - 1)
    stage_z(CH - 2, 2)
    w_hand_on(2)
    stage_m(CH - 1)
    stage_z(CH - 2, 3)
    for d in range(4):
        slot = ((x + 4 - d) % 4) * 2 + 1 - c
        arrived(wbuf.at[slot], w_recv.at[slot])
    stage_z(CH - 1, 0)

    def multiply(first, count, place):
        rows = 2 * RG * count
        block = abuf[place, first : first + count].reshape(rows, COLS)
        return jnp.dot(block, wbuf[place], preferred_element_type=F32).reshape(count, 2, RG, 512)

    for g in range(CH - 1):
        z_wait(g, 4)

    acc[...] = jnp.zeros_like(acc)

    def early(place, unused):
        acc[0 : CH - 1] += multiply(0, CH - 1, place)
        return unused

    lax.fori_loop(0, 4, early, 0)
    stage_z(CH - 1, 1)
    lax.fori_loop(4, 8, early, 0)
    stage_z(CH - 1, 2)
    for g in range(CH - 1):
        csend[g] = acc[g, 1 - yl].astype(BF16)

    def swap(n):
        some = pl.ds(0, CH - 1) if n == 0 else pl.ds(CH - 1, 1)
        return remote(csend.at[some], cbuf.at[some], c_send.at[n], c_recv.at[n], y_mate)

    swap(0).start()

    def late(d):
        acc[CH - 1 :] += multiply(CH - 1, 1, zz(d))

    late(0)
    late(-1)
    late(1)
    stage_z(CH - 1, 3)
    late(-2)
    late(2)
    late(-3)
    late(3)
    z_wait(CH - 1, 4)
    late(4)
    csend[CH - 1] = acc[CH - 1, 1 - yl].astype(BF16)
    swap(1).start()
    swap(0).wait_recv()
    for g in range(CH):
        if g == CH - 1:
            swap(1).wait_recv()
        out_ref[pl.ds(g * RG, RG), :] = (acc[g, yl] + cbuf[g].astype(F32)).astype(BF16)

    for n in range(2):
        swap(n).wait_send()
    for copy in kv_out:
        copy.wait_send()
    for d in range(4):
        w_forward(d).wait_send()
        if d > 0:
            w_copy(d).wait_send()

    def drain_chunk(g, unused):
        for n in range(1, 8):
            q_copy(g, n).wait_send()
        for a in range(2):
            @when(jnp.logical_not(m_is_self(a)))
            def _():
                m_copy(g, a).wait_send()

        for t in range(4):
            for way in range(2):
                z_copy(g, t, way).wait_send()
        return unused

    lax.fori_loop(0, CH, drain_chunk, 0)

    def drain_item(i, unused):
        reduce_y_start(i).wait_send()
        x_copy(i, 1).wait_send()

        @when(i % 2 == 1)
        def _():
            x_copy(i, 0).wait_send()

        return unused

    lax.fori_loop(0, 2 * CH, drain_item, 0)


def local(queries, cache_keys, cache_values, new_keys, new_values, out_weight):
    dma = pltpu.SemaphoreType.DMA
    hbm = pl.BlockSpec(memory_space=pltpu.HBM)
    vmem = pl.BlockSpec(memory_space=pltpu.VMEM)
    items = 2 * CH
    return pl.pallas_call(
        kernel,
        out_shape=jax.ShapeDtypeStruct((128, 512), BF16),
        in_specs=[vmem, hbm, hbm, hbm, hbm, hbm],
        out_specs=vmem,
        scratch_shapes=[
            pltpu.VMEM((KEYS, 2 * HD), BF16),
            pltpu.VMEM((KEYS, HD), BF16),
            pltpu.VMEM((VR, KEYS), BF16),
            pltpu.VMEM((KEYS, COLS), F32),
            pltpu.VMEM((8, 128, 512), BF16),
            pltpu.VMEM((2 * HD, COLS), BF16),
            pltpu.VMEM((2, VR, HALF), BF16),
            pltpu.VMEM((items, VR, HALF), BF16),
            pltpu.VMEM((items, VR, HALF), BF16),
            pltpu.VMEM((items, 2, VR, HD), BF16),
            pltpu.VMEM((CH, 4, VR, HD), BF16),
            pltpu.VMEM((CH, RG, 512), BF16),
            pltpu.VMEM((8, CH, 2, RG, 512), BF16),
            pltpu.VMEM((8, 512, 512), BF16),
            pltpu.VMEM((CH, 2, RG, 512), F32),
            pltpu.VMEM((CH, RG, 512), BF16),
            pltpu.VMEM((CH, RG, 512), BF16),
            dma((8,)), dma((6,)), dma((6,)), dma((CH, 8)), dma((CH, 8)),
            dma((4,)), dma((8,)), dma((4,)),
            dma((items,)), dma((items,)), dma((items, 2)), dma((CH, 4)),
            dma((CH, 2)), dma((CH, 2)), dma((CH, 4, 2)), dma((CH, 8)), dma((CH, 2)),
            dma((2,)), dma((2,)),
        ],
        compiler_params=pltpu.CompilerParams(
            collective_id=0, has_side_effects=True, vmem_limit_bytes=48 * 2**20
        ),
        cost_estimate=pl.CostEstimate(
            flops=11_000_000_000, bytes_accessed=4_000_000, transcendentals=18_000_000
        ),
    )(queries, cache_keys, cache_values, new_keys, new_values, out_weight)


def solution(mesh):
    placed = (
        P("seq", "head"),
        P("seq", None),
        P("seq", None),
        P("seq", None),
        P("seq", None),
        P("seq", "head"),
    )
    return jax.shard_map(
        local, mesh=mesh, in_specs=placed, out_specs=P("seq", "head"), check_vma=False
    )
```

```python
import functools

import jax
import jax.numpy as jnp
import numpy as np
from jax import lax
from jax.experimental import pallas as pl
from jax.experimental.pallas import tpu as pltpu
from jax.sharding import PartitionSpec as P

HD = 128
G = 4
CH = 4
RG = 128 // CH
COLS = 512
SHARD = 2048
CACHED = 2 * SHARD
KEYS = CACHED + 256
TK = 256
VR = 144
SCALE = float(HD**-0.5 * np.log2(np.e))
MESH = pl.DeviceIdType.MESH
F32, BF16 = jnp.float32, jnp.bfloat16


def pieces(row):
    a = row.astype(BF16).astype(F32)
    b = (row - a).astype(BF16).astype(F32)
    return [a, b, row - a - b]


def message(result, top, total):
    zeros = jnp.zeros((10, result.shape[1]), F32)
    tail = jnp.concatenate(pieces(top) + pieces(total) + [zeros], axis=0)
    return jnp.concatenate([result.astype(BF16), tail.astype(BF16)], axis=0)


def merge(messages):
    tops, totals = [], []
    for one in messages:
        tail = one[HD:].astype(F32)
        tops.append(tail[0:1] + tail[1:2] + tail[2:3])
        totals.append(tail[3:4] + tail[4:5] + tail[5:6])
    top = functools.reduce(jnp.maximum, tops)
    parts = [b * jnp.exp2(a - top) for a, b in zip(tops, totals)]
    total = functools.reduce(jnp.add, parts)
    result = functools.reduce(
        jnp.add, [one[:HD].astype(F32) * (part / total) for one, part in zip(messages, parts)]
    )
    return result


def kernel(
    q_ref, ck_ref, cv_ref, nk_ref, nv_ref, w_ref, out_ref,
    k2, vraw, vt, sbuf, qbuf, qt, osend, obuf, amine, abuf, wbuf, acc, csend, cbuf,
    loc_sem, kv_send, kv_recv, q_send, q_recv, w_send, w_recv, wf_send,
    o_send, o_recv, m_send, m_recv, z_send, z_recv, h_recv, c_send, c_recv,
):
    s = lax.axis_index("seq")
    h = lax.axis_index("head")
    yl, x, c = s // 8, (s // 2) % 4, s % 2
    yh, z = h // 8, h % 8
    me_block = yl * 4 + x
    partner = (s + 1 - 2 * c, h)

    def seq_of(a, b):
        return a * 8 + b * 2 + c

    y_mate = (seq_of(1 - yl, x), h)

    def remote(src, dst, ssem, rsem, dev):
        return pltpu.make_async_remote_copy(
            src_ref=src, dst_ref=dst, send_sem=ssem, recv_sem=rsem, device_id=dev, device_id_type=MESH
        )

    def arrived(ref, sem):
        pltpu.make_async_copy(ref, ref, sem).wait()

    kv_col = pl.ds(pl.multiple_of((h // 2) * HD, HD), HD)

    def cached_rows(core):
        return pl.ds(pl.multiple_of(core * SHARD, SHARD), SHARD)

    def new_rows(core):
        return pl.ds(pl.multiple_of(CACHED + core * 128, 128), 128)

    def kv_parts(core):
        return [
            (ck_ref.at[:, kv_col], k2.at[cached_rows(core), pl.ds(0, HD)]),
            (ck_ref.at[:, kv_col], k2.at[cached_rows(core), pl.ds(HD, HD)]),
            (nk_ref.at[:, kv_col], k2.at[new_rows(core), pl.ds(0, HD)]),
            (nk_ref.at[:, kv_col], k2.at[new_rows(core), pl.ds(HD, HD)]),
            (cv_ref.at[:, kv_col], vraw.at[cached_rows(core), :]),
            (nv_ref.at[:, kv_col], vraw.at[new_rows(core), :]),
        ]

    local = [
        pltpu.make_async_copy(src, dst, loc_sem.at[n]) for n, (src, dst) in enumerate(kv_parts(c))
    ]
    local.append(pltpu.make_async_copy(w_ref, wbuf.at[x * 2 + c], loc_sem.at[6]))
    local.append(pltpu.make_async_copy(q_ref, qbuf.at[me_block], loc_sem.at[7]))
    for copy in local:
        copy.start()

    barrier = pltpu.get_barrier_semaphore()

    def greet(dev):
        pl.semaphore_signal(barrier, inc=1, device_id=dev, device_id_type=MESH)

    def peer(n):
        return (seq_of((yl + n % 2) % 2, (x + n // 2) % 4), h)

    for n in range(1, 8):
        greet(peer(n))
    greet(partner)
    for d in (1, 2, 6, 7):
        greet((s, yh * 8 + (z + d) % 8))
        for a in range(2):
            greet((seq_of(a, x), yl * 8 + (z + d) % 8))
    for a in range(2):
        @pl.when(jnp.logical_or(yl != yh, yl != a))
        def _():
            greet((seq_of(a, x), yl * 8 + z))

    pl.semaphore_wait(barrier, jnp.where(yl == yh, 21, 22))

    kv_out = [
        remote(src, dst, kv_send.at[n], kv_recv.at[n], partner)
        for n, (src, dst) in enumerate(kv_parts(c))
    ]

    def q_copy(g, n):
        rows = pl.ds(pl.multiple_of(g * RG, RG), RG)
        return remote(
            q_ref.at[rows], qbuf.at[me_block, rows], q_send.at[g, n], q_recv.at[g, me_block], peer(n)
        )

    def q_start(g):
        for n in (1, 2, 6, 3, 7, 4, 5):
            q_copy(g, n).start()

    q_start(0)
    for copy in kv_out:
        copy.start()

    my_w = x * 2 + c

    def w_rows(j):
        return pl.ds(pl.multiple_of(j * 128, 128), 128)

    def w_copy(d, j):
        return remote(
            w_ref.at[w_rows(j)], wbuf.at[my_w, w_rows(j)], w_send.at[d, j], w_recv.at[my_w, j],
            (seq_of(yl, (x + d) % 4), h),
        )

    def w_start(j):
        for d in (1, 3, 2):
            w_copy(d, j).start()

    def w_forward(d):
        return remote(w_ref, wbuf.at[my_w], wf_send.at[0, 0], w_recv.at[my_w, 0], partner)

    def w_pass(d, j):
        slot = ((x + 4 - d) % 4) * 2 + c
        ref = wbuf.at[slot, w_rows(j)]
        return remote(ref, ref, wf_send.at[d, j], w_recv.at[slot, j], partner)

    def w_hand_on(j):
        for d in (1, 3, 2):
            slot = ((x + 4 - d) % 4) * 2 + c
            arrived(wbuf.at[slot, w_rows(j)], w_recv.at[slot, j])
            w_pass(d, j).start()

    def flip(rows):
        vt[pl.ds(0, HD), rows] = vraw[rows, :].T

    def flip_cached(core):
        def one(t, unused):
            flip(pl.ds(pl.multiple_of(core * SHARD + t * TK, TK), TK))
            return unused

        lax.fori_loop(0, SHARD // TK, one, 0)

    vt[pl.ds(HD, VR - HD), :] = jnp.ones((VR - HD, KEYS), BF16)
    for copy in local:
        copy.wait()
    flip_cached(c)

    def o_place(i, n):
        return (yl + n // 2) % 2, (x + 2 * (i % 2) + n % 2) % 4

    def o_copy(i, n):
        p, q = o_place(i, n)
        return remote(
            osend.at[i, n], obuf.at[i // 2, me_block], o_send.at[i, n], o_recv.at[i // 2, me_block],
            (seq_of(p, q), h),
        )

    def stage_o(i):
        for n in (2, 1, 3):
            o_copy(i, n).start()

        @pl.when(i % 2 == 0)
        def _():
            pltpu.make_async_copy(
                osend.at[i, 0], obuf.at[i // 2, me_block], o_recv.at[i // 2, me_block]
            ).start()

        @pl.when(i % 2 == 1)
        def _():
            o_copy(i, 0).start()

    def zz(d):
        return (z + 8 + d) % 8

    def m_copy(g, a, d):
        return remote(
            amine.at[g], abuf.at[z, g, yl], m_send.at[g, a, d + 2], m_recv.at[g, z, yl],
            (seq_of(yh, x), a * 8 + zz(d)),
        )

    def m_is_self(a):
        return jnp.logical_and(yl == yh, yh == a)

    def stage_m(g):
        for j in range(8):
            arrived(obuf.at[g, j], o_recv.at[g, j])
        result = merge([obuf[g, j] for j in range(8)])
        turned = result.T.astype(BF16)
        for n in range(G):
            amine[g, :, pl.ds(n * HD, HD)] = turned[n * RG : (n + 1) * RG]
        for d in (-2, 2, -1, 1):
            for a in range(2):
                m_copy(g, a, d).start()
        for a in range(2):
            @pl.when(m_is_self(a))
            def _():
                pltpu.make_async_copy(amine.at[g], abuf.at[z, g, yl], m_recv.at[g, z, yl]).start()

            @pl.when(jnp.logical_not(m_is_self(a)))
            def _():
                m_copy(g, a, 0).start()

    def m_wait(g, d):
        for a in range(2):
            arrived(abuf.at[zz(d), g, a], m_recv.at[g, zz(d), a])

    def z_copies(g):
        near, far = abuf.at[zz(-2), g], abuf.at[zz(2), g]
        half, other = abuf.at[zz(-2), g, 0], abuf.at[zz(2), g, 1]
        return (
            remote(half, half, z_send.at[g, 0], h_recv.at[g, 0], (s, yh * 8 + zz(2))),
            remote(other, other, z_send.at[g, 1], h_recv.at[g, 1], (s, yh * 8 + zz(-2))),
            remote(near, near, z_send.at[g, 2], z_recv.at[g, 0], (s, yh * 8 + zz(1))),
            remote(far, far, z_send.at[g, 3], z_recv.at[g, 1], (s, yh * 8 + zz(-1))),
        )

    def stage_z(g):
        m_wait(g, -2)
        m_wait(g, 2)
        for copy in z_copies(g):
            copy.start()

    def z_wait(g):
        for d in (-1, 0, 1):
            m_wait(g, d)
        arrived(abuf.at[zz(-3), g], z_recv.at[g, 0])
        arrived(abuf.at[zz(3), g], z_recv.at[g, 1])
        for a in range(2):
            arrived(abuf.at[zz(4), g, a], h_recv.at[g, a])

    def one_item(i, unused):
        g, sub = i // 2, i % 2
        places = [((yl + dy) % 2, (x + 2 * sub + k) % 4) for dy in range(2) for k in range(2)]

        @pl.when(jnp.logical_and(sub == 0, g < CH - 1))
        def _():
            q_start(g + 1)

        rows = pl.ds(pl.multiple_of(g * RG, RG), RG)
        for n, (a, b) in enumerate(places):
            block = a * 4 + b
            if n == 0:
                @pl.when(sub > 0)
                def _():
                    arrived(qbuf.at[block, rows], q_recv.at[g, block])
            else:
                arrived(qbuf.at[block, rows], q_recv.at[g, block])
        tall = jnp.concatenate(
            [qbuf[a * 4 + b, rows, pl.ds(n * HD, HD)] for a, b in places for n in range(G)], axis=0
        )
        wide = tall.astype(F32).T * SCALE
        high = wide.astype(BF16)
        qt[pl.ds(0, HD), :] = high
        qt[pl.ds(HD, HD), :] = (wide - high.astype(F32)).astype(BF16)

        def score(rows):
            return jnp.dot(k2[rows, :], qt[...], preferred_element_type=F32)

        def highest(top, scores):
            return jnp.maximum(top, jnp.max(scores.reshape(TK // 8, 8, COLS), axis=0))

        top = jnp.full((8, COLS), -1e30, F32)
        for core in (c, 1 - c):
            for t in range(SHARD // TK):
                rows = pl.ds(pl.multiple_of(core * SHARD + t * TK, TK), TK)
                scores = score(rows)
                sbuf[rows, :] = scores
                top = highest(top, scores)
            if core is c:
                @pl.when(i == 0)
                def _():
                    for copy in kv_out[:4]:
                        copy.wait_recv()

        col = lax.broadcasted_iota(jnp.int32, (1, COLS), 1)
        base = jnp.zeros((1, COLS), jnp.int32)
        for n, (a, b) in enumerate(places):
            base = jnp.where(col // HD == n, seq_of(a, b) * 128, base)
        query_pos = base + g * RG + col % RG
        rows = pl.ds(CACHED, TK)
        key_pos = (yl * 8 + x * 2) * 128 + lax.broadcasted_iota(jnp.int32, (TK, COLS), 0)
        scores = jnp.where(key_pos <= query_pos, score(rows), -1e30)
        sbuf[rows, :] = scores
        top = jnp.max(highest(top, scores), axis=0, keepdims=True)

        @pl.when(i == 0)
        def _():
            for copy in kv_out[4:]:
                copy.wait_recv()
            flip_cached(1 - c)
            flip(pl.ds(CACHED, 256))

        @pl.when(jnp.logical_and(sub == 1, i >= 3))
        def _():
            stage_m((i - 3) // 2)

        summed = jnp.zeros((VR, COLS), F32)
        for t in range(KEYS // TK):
            weights = jnp.exp2(sbuf[pl.ds(t * TK, TK), :] - top).astype(BF16)
            summed = summed + jnp.dot(vt[:, pl.ds(t * TK, TK)], weights, preferred_element_type=F32)
        total = summed[HD : HD + 1]
        packed = message(summed[:HD] / total, top, total)
        for n in range(4):
            osend[i, n] = packed[:, n * HD : (n + 1) * HD]
        stage_o(i)

        @pl.when(jnp.logical_and(sub == 0, i >= 4))
        def _():
            stage_z((i - 4) // 2)

        @pl.when(i == 0)
        def _():
            w_forward(0).start()

        @pl.when(jnp.logical_and(sub == 1, i < 6))
        def _():
            w_start(i // 2)

        @pl.when(jnp.logical_and(sub == 0, i >= 4))
        def _():
            w_hand_on((i - 4) // 2)

        return unused

    lax.fori_loop(0, 2 * CH, one_item, 0)

    stage_m(CH - 1)
    w_start(3)
    stage_z(CH - 2)
    w_hand_on(2)
    stage_z(CH - 1)
    w_hand_on(3)
    for g in range(CH - 1):
        z_wait(g)
    slot = my_w + 1 - 2 * c
    arrived(wbuf.at[slot], w_recv.at[slot, 0])
    for j in range(4):
        for d in (1, 3, 2):
            slot = ((x + 4 - d) % 4) * 2 + 1 - c
            arrived(wbuf.at[slot, w_rows(j)], w_recv.at[slot, j])

    def multiply(first, count, place):
        rows = 2 * RG * count
        block = abuf[place, first : first + count].reshape(rows, COLS)
        return jnp.dot(block, wbuf[place], preferred_element_type=F32).reshape(count, 2, RG, 512)

    acc[...] = jnp.zeros_like(acc)

    def early(place, unused):
        acc[0 : CH - 1] += multiply(0, CH - 1, place)
        return unused

    lax.fori_loop(0, 8, early, 0)
    for g in range(CH - 1):
        csend[g] = acc[g, 1 - yl].astype(BF16)

    def swap(n):
        some = pl.ds(0, CH - 1) if n == 0 else pl.ds(CH - 1, 1)
        return remote(csend.at[some], cbuf.at[some], c_send.at[n], c_recv.at[n], y_mate)

    swap(0).start()

    def late(d):
        acc[CH - 1 :] += multiply(CH - 1, 1, zz(d))

    z_wait(CH - 1)
    for d in range(8):
        late(d - 4)
    csend[CH - 1] = acc[CH - 1, 1 - yl].astype(BF16)
    swap(1).start()
    swap(0).wait_recv()
    for g in range(CH):
        if g == CH - 1:
            swap(1).wait_recv()
        out_ref[pl.ds(g * RG, RG), :] = (acc[g, yl] + cbuf[g].astype(F32)).astype(BF16)

    for n in range(2):
        swap(n).wait_send()
    for copy in kv_out:
        copy.wait_send()
    w_forward(0).wait_send()
    for d in range(1, 4):
        for j in range(4):
            w_copy(d, j).wait_send()
            w_pass(d, j).wait_send()

    def drain_chunk(g, unused):
        for n in range(1, 8):
            q_copy(g, n).wait_send()
        for a in range(2):
            for d in (-2, -1, 1, 2):
                m_copy(g, a, d).wait_send()

            @pl.when(jnp.logical_not(m_is_self(a)))
            def _():
                m_copy(g, a, 0).wait_send()

        for copy in z_copies(g):
            copy.wait_send()
        return unused

    lax.fori_loop(0, CH, drain_chunk, 0)

    def drain_item(i, unused):
        for n in range(1, 4):
            o_copy(i, n).wait_send()

        @pl.when(i % 2 == 1)
        def _():
            o_copy(i, 0).wait_send()

        return unused

    lax.fori_loop(0, 2 * CH, drain_item, 0)


def local(queries, cache_keys, cache_values, new_keys, new_values, out_weight):
    dma = pltpu.SemaphoreType.DMA
    hbm = pl.BlockSpec(memory_space=pltpu.HBM)
    vmem = pl.BlockSpec(memory_space=pltpu.VMEM)
    items = 2 * CH
    return pl.pallas_call(
        kernel,
        out_shape=jax.ShapeDtypeStruct((128, 512), BF16),
        in_specs=[vmem, hbm, hbm, hbm, hbm, hbm],
        out_specs=vmem,
        scratch_shapes=[
            pltpu.VMEM((KEYS, 2 * HD), BF16),
            pltpu.VMEM((KEYS, HD), BF16),
            pltpu.VMEM((VR, KEYS), BF16),
            pltpu.VMEM((KEYS, COLS), F32),
            pltpu.VMEM((8, 128, 512), BF16),
            pltpu.VMEM((2 * HD, COLS), BF16),
            pltpu.VMEM((items, 4, VR, HD), BF16),
            pltpu.VMEM((CH, 8, VR, HD), BF16),
            pltpu.VMEM((CH, RG, 512), BF16),
            pltpu.VMEM((8, CH, 2, RG, 512), BF16),
            pltpu.VMEM((8, 512, 512), BF16),
            pltpu.VMEM((CH, 2, RG, 512), F32),
            pltpu.VMEM((CH, RG, 512), BF16),
            pltpu.VMEM((CH, RG, 512), BF16),
            dma((8,)), dma((6,)), dma((6,)), dma((CH, 8)), dma((CH, 8)),
            dma((4, 4)), dma((8, 4)), dma((4, 4)),
            dma((items, 4)), dma((CH, 8)),
            dma((CH, 2, 5)), dma((CH, 8, 2)), dma((CH, 4)), dma((CH, 2)), dma((CH, 2)),
            dma((2,)), dma((2,)),
        ],
        compiler_params=pltpu.CompilerParams(
            collective_id=0, has_side_effects=True, vmem_limit_bytes=60 * 2**20
        ),
        cost_estimate=pl.CostEstimate(
            flops=11_000_000_000, bytes_accessed=4_000_000, transcendentals=18_000_000
        ),
    )(queries, cache_keys, cache_values, new_keys, new_values, out_weight)


def solution(mesh):
    placed = (
        P("seq", "head"),
        P("seq", None),
        P("seq", None),
        P("seq", None),
        P("seq", None),
        P("seq", "head"),
    )
    return jax.shard_map(
        local, mesh=mesh, in_specs=placed, out_specs=P("seq", "head"), check_vma=False
    )
```

```python
import functools

import jax
import jax.numpy as jnp
import numpy as np
from jax import lax
from jax.experimental import pallas as pl
from jax.experimental.pallas import tpu as pltpu
from jax.sharding import PartitionSpec as P

HD = 128
G = 4
CH = 4
RG = 128 // CH
COLS = 512
SHARD = 2048
CACHED = 2 * SHARD
KEYS = CACHED + 256
TK = 256
VR = 144
SCALE = float(HD**-0.5 * np.log2(np.e))
MESH = pl.DeviceIdType.MESH
F32, BF16 = jnp.float32, jnp.bfloat16


def pieces(row):
    a = row.astype(BF16).astype(F32)
    b = (row - a).astype(BF16).astype(F32)
    return [a, b, row - a - b]


def message(result, top, total):
    zeros = jnp.zeros((10, result.shape[1]), F32)
    tail = jnp.concatenate(pieces(top) + pieces(total) + [zeros], axis=0)
    return jnp.concatenate([result.astype(BF16), tail.astype(BF16)], axis=0)


def merge(messages):
    tops, totals = [], []
    for one in messages:
        tail = one[HD:].astype(F32)
        tops.append(tail[0:1] + tail[1:2] + tail[2:3])
        totals.append(tail[3:4] + tail[4:5] + tail[5:6])
    top = functools.reduce(jnp.maximum, tops)
    parts = [b * jnp.exp2(a - top) for a, b in zip(tops, totals)]
    total = functools.reduce(jnp.add, parts)
    result = functools.reduce(
        jnp.add, [one[:HD].astype(F32) * (part / total) for one, part in zip(messages, parts)]
    )
    return result


def kernel(
    q_ref, ck_ref, cv_ref, nk_ref, nv_ref, w_ref, out_ref,
    k2, vraw, vt, sbuf, qbuf, qt, osend, obuf, amine, abuf, wbuf, acc, csend, cbuf,
    loc_sem, kv_send, kv_recv, q_send, q_recv, w_send, w_recv, wf_send,
    o_send, o_recv, m_send, m_recv, z_send, z_recv, c_send, c_recv,
):
    s = lax.axis_index("seq")
    h = lax.axis_index("head")
    yl, x, c = s // 8, (s // 2) % 4, s % 2
    yh, z = h // 8, h % 8
    me_block = yl * 4 + x
    partner = (s + 1 - 2 * c, h)

    def seq_of(a, b):
        return a * 8 + b * 2 + c

    y_mate = (seq_of(1 - yl, x), h)

    def remote(src, dst, ssem, rsem, dev):
        return pltpu.make_async_remote_copy(
            src_ref=src, dst_ref=dst, send_sem=ssem, recv_sem=rsem, device_id=dev, device_id_type=MESH
        )

    def arrived(ref, sem):
        pltpu.make_async_copy(ref, ref, sem).wait()

    kv_col = pl.ds(pl.multiple_of((h // 2) * HD, HD), HD)

    def cached_rows(core):
        return pl.ds(pl.multiple_of(core * SHARD, SHARD), SHARD)

    def new_rows(core):
        return pl.ds(pl.multiple_of(CACHED + core * 128, 128), 128)

    def kv_parts(core):
        return [
            (ck_ref.at[:, kv_col], k2.at[cached_rows(core), pl.ds(0, HD)]),
            (ck_ref.at[:, kv_col], k2.at[cached_rows(core), pl.ds(HD, HD)]),
            (nk_ref.at[:, kv_col], k2.at[new_rows(core), pl.ds(0, HD)]),
            (nk_ref.at[:, kv_col], k2.at[new_rows(core), pl.ds(HD, HD)]),
            (cv_ref.at[:, kv_col], vraw.at[cached_rows(core), :]),
            (nv_ref.at[:, kv_col], vraw.at[new_rows(core), :]),
        ]

    local = [
        pltpu.make_async_copy(src, dst, loc_sem.at[n]) for n, (src, dst) in enumerate(kv_parts(c))
    ]
    local.append(pltpu.make_async_copy(w_ref, wbuf.at[x * 2 + c], loc_sem.at[6]))
    local.append(pltpu.make_async_copy(q_ref, qbuf.at[me_block], loc_sem.at[7]))
    for copy in local:
        copy.start()

    barrier = pltpu.get_barrier_semaphore()

    def greet(dev):
        pl.semaphore_signal(barrier, inc=1, device_id=dev, device_id_type=MESH)

    def peer(n):
        return (seq_of((yl + n % 2) % 2, (x + n // 2) % 4), h)

    for n in range(1, 8):
        greet(peer(n))
    greet(partner)
    for d in (1, 2, 6, 7):
        greet((s, yh * 8 + (z + d) % 8))
    for a in range(2):
        greet((seq_of(a, x), yl * 8 + (z + 4) % 8))
    for a in range(2):
        @pl.when(jnp.logical_or(yl != yh, yl != a))
        def _():
            greet((seq_of(a, x), yl * 8 + z))

    pl.semaphore_wait(barrier, jnp.where(yl == yh, 15, 16))

    kv_out = [
        remote(src, dst, kv_send.at[n], kv_recv.at[n], partner)
        for n, (src, dst) in enumerate(kv_parts(c))
    ]

    def q_copy(g, n):
        rows = pl.ds(pl.multiple_of(g * RG, RG), RG)
        return remote(
            q_ref.at[rows], qbuf.at[me_block, rows], q_send.at[g, n], q_recv.at[g, me_block], peer(n)
        )

    def q_start(g):
        for n in (1, 2, 6, 3, 7, 4, 5):
            q_copy(g, n).start()

    q_start(0)
    for copy in kv_out:
        copy.start()

    my_w = x * 2 + c

    def w_rows(j):
        return pl.ds(pl.multiple_of(j * 128, 128), 128)

    def w_copy(d, j):
        return remote(
            w_ref.at[w_rows(j)], wbuf.at[my_w, w_rows(j)], w_send.at[d, j], w_recv.at[my_w, j],
            (seq_of(yl, (x + d) % 4), h),
        )

    def w_start(j):
        w_copy(1, j).start()
        w_copy(3, j).start()

    def w_on(j):
        step = 1 + 2 * (j % 2)
        slot = ((x + 4 - step) % 4) * 2 + c
        ref = wbuf.at[slot, w_rows(j)]
        return remote(
            ref, ref, w_send.at[2, j], w_recv.at[slot, j], (seq_of(yl, (x + step) % 4), h)
        )

    def w_forward(d):
        return remote(w_ref, wbuf.at[my_w], wf_send.at[0, 0], w_recv.at[my_w, 0], partner)

    def w_pass(d, j):
        slot = ((x + 4 - d) % 4) * 2 + c
        ref = wbuf.at[slot, w_rows(j)]
        return remote(ref, ref, wf_send.at[d, j], w_recv.at[slot, j], partner)

    def w_far(d, j):
        slot = ((x + 4 - d) % 4) * 2 + c
        arrived(wbuf.at[slot, w_rows(j)], w_recv.at[slot, j])

    def w_hand_on(j, last=False):
        w_far(1, j)
        w_far(3, j)
        if not last:
            w_on(j).start()
        w_pass(1, j).start()
        w_pass(3, j).start()

    def w_hand_far(j):
        w_far(2, j)
        w_pass(2, j).start()

    def w_partner(j):
        for d in (1, 3, 2):
            slot = ((x + 4 - d) % 4) * 2 + 1 - c
            arrived(wbuf.at[slot, w_rows(j)], w_recv.at[slot, j])

    def flip(rows):
        vt[pl.ds(0, HD), rows] = vraw[rows, :].T

    def flip_cached(core):
        def one(t, unused):
            flip(pl.ds(pl.multiple_of(core * SHARD + t * TK, TK), TK))
            return unused

        lax.fori_loop(0, SHARD // TK, one, 0)

    vt[pl.ds(HD, VR - HD), :] = jnp.ones((VR - HD, KEYS), BF16)
    for copy in local:
        copy.wait()
    flip_cached(c)

    def o_place(i, n):
        return (yl + n // 2) % 2, (x + 2 * (i % 2) + n % 2) % 4

    def o_copy(i, n):
        p, q = o_place(i, n)
        return remote(
            osend.at[i, n], obuf.at[i // 2, me_block], o_send.at[i, n], o_recv.at[i // 2, me_block],
            (seq_of(p, q), h),
        )

    def stage_o(i):
        for n in (2, 1, 3):
            o_copy(i, n).start()

        @pl.when(i % 2 == 0)
        def _():
            pltpu.make_async_copy(
                osend.at[i, 0], obuf.at[i // 2, me_block], o_recv.at[i // 2, me_block]
            ).start()

        @pl.when(i % 2 == 1)
        def _():
            o_copy(i, 0).start()

    def zz(d):
        return (z + 8 + d) % 8

    def m_copy(g, a, far):
        return remote(
            amine.at[g], abuf.at[z, g, yl], m_send.at[g, a, far], m_recv.at[g, far, yl],
            (seq_of(yh, x), a * 8 + zz(4 * far)),
        )

    def m_is_self(a):
        return jnp.logical_and(yl == yh, yh == a)

    def stage_m(g):
        for j in range(8):
            arrived(obuf.at[g, j], o_recv.at[g, j])
        result = merge([obuf[g, j] for j in range(8)])
        turned = result.T.astype(BF16)
        for n in range(G):
            amine[g, :, pl.ds(n * HD, HD)] = turned[n * RG : (n + 1) * RG]
        for a in range(2):
            m_copy(g, a, 1).start()
        for a in range(2):
            @pl.when(m_is_self(a))
            def _():
                pltpu.make_async_copy(amine.at[g], abuf.at[z, g, yl], m_recv.at[g, 0, yl]).start()

            @pl.when(jnp.logical_not(m_is_self(a)))
            def _():
                m_copy(g, a, 0).start()

    def z_copies(g):
        near, far = abuf.at[z, g], abuf.at[zz(4), g]
        plan = ((near, 2), (near, -2), (far, 1), (far, -1), (near, 1), (near, -1))
        return [
            remote(ref, ref, z_send.at[g, n], z_recv.at[g, n], (s, yh * 8 + zz(d)))
            for n, (ref, d) in enumerate(plan)
        ]

    def stage_z(g):
        for a in range(2):
            arrived(abuf.at[z, g, a], m_recv.at[g, 0, a])
            arrived(abuf.at[zz(4), g, a], m_recv.at[g, 1, a])
        for copy in z_copies(g):
            copy.start()

    def z_wait(g):
        for n, d in enumerate((-2, 2, 3, -3, -1, 1)):
            arrived(abuf.at[zz(d), g], z_recv.at[g, n])

    def one_item(i, unused):
        g, sub = i // 2, i % 2
        places = [((yl + dy) % 2, (x + 2 * sub + k) % 4) for dy in range(2) for k in range(2)]

        @pl.when(jnp.logical_and(sub == 0, g < CH - 1))
        def _():
            q_start(g + 1)

        rows = pl.ds(pl.multiple_of(g * RG, RG), RG)
        for n, (a, b) in enumerate(places):
            block = a * 4 + b
            if n == 0:
                @pl.when(sub > 0)
                def _():
                    arrived(qbuf.at[block, rows], q_recv.at[g, block])
            else:
                arrived(qbuf.at[block, rows], q_recv.at[g, block])
        tall = jnp.concatenate(
            [qbuf[a * 4 + b, rows, pl.ds(n * HD, HD)] for a, b in places for n in range(G)], axis=0
        )
        wide = tall.astype(F32).T * SCALE
        high = wide.astype(BF16)
        qt[pl.ds(0, HD), :] = high
        qt[pl.ds(HD, HD), :] = (wide - high.astype(F32)).astype(BF16)

        def score(rows):
            return jnp.dot(k2[rows, :], qt[...], preferred_element_type=F32)

        def highest(top, scores):
            return jnp.maximum(top, jnp.max(scores.reshape(TK // 8, 8, COLS), axis=0))

        top = jnp.full((8, COLS), -1e30, F32)
        for core in (c, 1 - c):
            for t in range(SHARD // TK):
                rows = pl.ds(pl.multiple_of(core * SHARD + t * TK, TK), TK)
                scores = score(rows)
                sbuf[rows, :] = scores
                top = highest(top, scores)
            if core is c:
                @pl.when(i == 0)
                def _():
                    for copy in kv_out[:4]:
                        copy.wait_recv()

        col = lax.broadcasted_iota(jnp.int32, (1, COLS), 1)
        base = jnp.zeros((1, COLS), jnp.int32)
        for n, (a, b) in enumerate(places):
            base = jnp.where(col // HD == n, seq_of(a, b) * 128, base)
        query_pos = base + g * RG + col % RG
        rows = pl.ds(CACHED, TK)
        key_pos = (yl * 8 + x * 2) * 128 + lax.broadcasted_iota(jnp.int32, (TK, COLS), 0)
        scores = jnp.where(key_pos <= query_pos, score(rows), -1e30)
        sbuf[rows, :] = scores
        top = jnp.max(highest(top, scores), axis=0, keepdims=True)

        @pl.when(i == 0)
        def _():
            for copy in kv_out[4:]:
                copy.wait_recv()
            flip_cached(1 - c)
            flip(pl.ds(CACHED, 256))

        @pl.when(jnp.logical_and(sub == 1, i >= 3))
        def _():
            stage_m((i - 3) // 2)

        summed = jnp.zeros((VR, COLS), F32)
        for t in range(KEYS // TK):
            weights = jnp.exp2(sbuf[pl.ds(t * TK, TK), :] - top).astype(BF16)
            summed = summed + jnp.dot(vt[:, pl.ds(t * TK, TK)], weights, preferred_element_type=F32)
        total = summed[HD : HD + 1]
        packed = message(summed[:HD] / total, top, total)
        for n in range(4):
            osend[i, n] = packed[:, n * HD : (n + 1) * HD]
        stage_o(i)

        @pl.when(jnp.logical_and(sub == 0, i >= 4))
        def _():
            stage_z((i - 4) // 2)

        @pl.when(i == 0)
        def _():
            w_forward(0).start()

        @pl.when(jnp.logical_and(sub == 0, i < 6))
        def _():
            w_start(i // 2)

        @pl.when(jnp.logical_and(sub == 1, i >= 3))
        def _():
            w_hand_on((i - 3) // 2)

        @pl.when(jnp.logical_and(sub == 1, i >= 5))
        def _():
            w_hand_far((i - 5) // 2)

        return unused

    lax.fori_loop(0, 2 * CH, one_item, 0)

    def multiply(first, count, place, low, high):
        rows = 2 * RG * count
        block = abuf[place, first : first + count].reshape(rows, 512)
        product = jnp.dot(
            block[:, low:high], wbuf[place, pl.ds(low, high - low), :], preferred_element_type=F32
        )
        acc[first : first + count] += product.reshape(count, 2, RG, 512)

    stage_m(CH - 1)
    w_start(3)
    w_copy(2, 3).start()
    stage_z(CH - 2)
    w_hand_far(2)
    acc[...] = jnp.zeros_like(acc)

    def drain_item(i, unused):
        for n in range(1, 4):
            o_copy(i, n).wait_send()

        @pl.when(i % 2 == 1)
        def _():
            o_copy(i, 0).wait_send()

        return unused

    lax.fori_loop(0, 2 * CH, drain_item, 0)
    for g in range(CH - 2):
        z_wait(g)
    slot = my_w + 1 - 2 * c
    arrived(wbuf.at[slot], w_recv.at[slot, 0])
    for j in range(3):
        w_partner(j)

    def first_part(place, unused):
        multiply(0, CH - 2, place, 0, 384)
        return unused

    lax.fori_loop(0, 8, first_part, 0)
    stage_z(CH - 1)
    w_hand_on(3, last=True)
    w_hand_far(3)

    def drain_chunk(g, unused):
        for n in range(1, 8):
            q_copy(g, n).wait_send()
        for a in range(2):
            m_copy(g, a, 1).wait_send()

            @pl.when(jnp.logical_not(m_is_self(a)))
            def _():
                m_copy(g, a, 0).wait_send()

        return unused

    lax.fori_loop(0, CH, drain_chunk, 0)
    z_wait(CH - 2)
    w_partner(3)

    def second_part(place, unused):
        multiply(0, CH - 2, place, 384, 512)
        multiply(CH - 2, 1, place, 0, 512)
        return unused

    lax.fori_loop(0, 8, second_part, 0)
    for g in range(CH - 1):
        csend[g] = acc[g, 1 - yl].astype(BF16)

    def swap(n):
        some = pl.ds(0, CH - 1) if n == 0 else pl.ds(CH - 1, 1)
        return remote(csend.at[some], cbuf.at[some], c_send.at[n], c_recv.at[n], y_mate)

    swap(0).start()

    for copy in kv_out:
        copy.wait_send()
    w_forward(0).wait_send()
    for j in range(4):
        for d in range(1, 4):
            if d == 2 and j < 3:
                w_on(j).wait_send()
            else:
                w_copy(d, j).wait_send()
            w_pass(d, j).wait_send()
    for g in range(CH - 1):
        for copy in z_copies(g):
            copy.wait_send()

    def last_part(place, unused):
        multiply(CH - 1, 1, place, 0, 512)
        return unused

    z_wait(CH - 1)
    lax.fori_loop(0, 8, last_part, 0)
    csend[CH - 1] = acc[CH - 1, 1 - yl].astype(BF16)
    swap(1).start()
    swap(0).wait_recv()
    for g in range(CH):
        if g == CH - 1:
            swap(1).wait_recv()
        out_ref[pl.ds(g * RG, RG), :] = (acc[g, yl] + cbuf[g].astype(F32)).astype(BF16)

    for n in range(2):
        swap(n).wait_send()
    for copy in z_copies(CH - 1):
        copy.wait_send()


def local(queries, cache_keys, cache_values, new_keys, new_values, out_weight):
    dma = pltpu.SemaphoreType.DMA
    hbm = pl.BlockSpec(memory_space=pltpu.HBM)
    vmem = pl.BlockSpec(memory_space=pltpu.VMEM)
    items = 2 * CH
    return pl.pallas_call(
        kernel,
        out_shape=jax.ShapeDtypeStruct((128, 512), BF16),
        in_specs=[vmem, hbm, hbm, hbm, hbm, hbm],
        out_specs=vmem,
        scratch_shapes=[
            pltpu.VMEM((KEYS, 2 * HD), BF16),
            pltpu.VMEM((KEYS, HD), BF16),
            pltpu.VMEM((VR, KEYS), BF16),
            pltpu.VMEM((KEYS, COLS), F32),
            pltpu.VMEM((8, 128, 512), BF16),
            pltpu.VMEM((2 * HD, COLS), BF16),
            pltpu.VMEM((items, 4, VR, HD), BF16),
            pltpu.VMEM((CH, 8, VR, HD), BF16),
            pltpu.VMEM((CH, RG, 512), BF16),
            pltpu.VMEM((8, CH, 2, RG, 512), BF16),
            pltpu.VMEM((8, 512, 512), BF16),
            pltpu.VMEM((CH, 2, RG, 512), F32),
            pltpu.VMEM((CH, RG, 512), BF16),
            pltpu.VMEM((CH, RG, 512), BF16),
            dma((8,)), dma((6,)), dma((6,)), dma((CH, 8)), dma((CH, 8)),
            dma((4, 4)), dma((8, 4)), dma((4, 4)),
            dma((items, 4)), dma((CH, 8)),
            dma((CH, 2, 2)), dma((CH, 2, 2)), dma((CH, 6)), dma((CH, 6)),
            dma((2,)), dma((2,)),
        ],
        compiler_params=pltpu.CompilerParams(
            collective_id=0, has_side_effects=True, vmem_limit_bytes=60 * 2**20
        ),
        cost_estimate=pl.CostEstimate(
            flops=11_000_000_000, bytes_accessed=4_000_000, transcendentals=18_000_000
        ),
    )(queries, cache_keys, cache_values, new_keys, new_values, out_weight)


def solution(mesh):
    placed = (
        P("seq", "head"),
        P("seq", None),
        P("seq", None),
        P("seq", None),
        P("seq", None),
        P("seq", "head"),
    )
    return jax.shard_map(
        local, mesh=mesh, in_specs=placed, out_specs=P("seq", "head"), check_vma=False
    )
```

```python
import functools

import jax
import jax.numpy as jnp
import numpy as np
from jax import lax
from jax.experimental import pallas as pl
from jax.experimental.pallas import tpu as pltpu
from jax.sharding import PartitionSpec as P

HD = 128
G = 4
CH = 4
RG = 128 // CH
COLS = 512
SHARD = 2048
CACHED = 2 * SHARD
KEYS = CACHED + 256
TK = 256
VR = 144
SCALE = float(HD**-0.5 * np.log2(np.e))
MESH = pl.DeviceIdType.MESH
F32, BF16 = jnp.float32, jnp.bfloat16


def pieces(row):
    a = row.astype(BF16).astype(F32)
    b = (row - a).astype(BF16).astype(F32)
    return [a, b, row - a - b]


def message(result, top, total):
    zeros = jnp.zeros((10, result.shape[1]), F32)
    tail = jnp.concatenate(pieces(top) + pieces(total) + [zeros], axis=0)
    return jnp.concatenate([result.astype(BF16), tail.astype(BF16)], axis=0)


def merge(messages):
    tops, totals = [], []
    for one in messages:
        tail = one[HD:].astype(F32)
        tops.append(tail[0:1] + tail[1:2] + tail[2:3])
        totals.append(tail[3:4] + tail[4:5] + tail[5:6])
    top = functools.reduce(jnp.maximum, tops)
    parts = [b * jnp.exp2(a - top) for a, b in zip(tops, totals)]
    total = functools.reduce(jnp.add, parts)
    result = functools.reduce(
        jnp.add, [one[:HD].astype(F32) * (part / total) for one, part in zip(messages, parts)]
    )
    return result


def kernel(
    q_ref, ck_ref, cv_ref, nk_ref, nv_ref, w_ref, out_ref,
    keys, vraw, vt, sbuf, qbuf, qt, osend, obuf, amine, abuf, wbuf, acc, csend, cbuf,
    loc_sem, kv_send, kv_recv, q_send, q_recv, w_send, w_recv, wf_send,
    o_send, o_recv, m_send, m_recv, z_send, z_recv, c_send, c_recv,
):
    s = lax.axis_index("seq")
    h = lax.axis_index("head")
    yl, x, c = s // 8, (s // 2) % 4, s % 2
    yh, z = h // 8, h % 8
    me_block = yl * 4 + x
    partner = (s + 1 - 2 * c, h)

    def seq_of(a, b):
        return a * 8 + b * 2 + c

    y_mate = (seq_of(1 - yl, x), h)

    def remote(src, dst, ssem, rsem, dev):
        return pltpu.make_async_remote_copy(
            src_ref=src, dst_ref=dst, send_sem=ssem, recv_sem=rsem, device_id=dev, device_id_type=MESH
        )

    def arrived(ref, sem):
        pltpu.make_async_copy(ref, ref, sem).wait()

    kv_col = pl.ds(pl.multiple_of((h // 2) * HD, HD), HD)

    def cached_rows(core):
        return pl.ds(pl.multiple_of(core * SHARD, SHARD), SHARD)

    def new_rows(core):
        return pl.ds(pl.multiple_of(CACHED + core * 128, 128), 128)

    def kv_parts(core):
        return [
            (ck_ref.at[:, kv_col], keys.at[cached_rows(core), :]),
            (nk_ref.at[:, kv_col], keys.at[new_rows(core), :]),
            (cv_ref.at[:, kv_col], vraw.at[cached_rows(core), :]),
            (nv_ref.at[:, kv_col], vraw.at[new_rows(core), :]),
        ]

    local = [
        pltpu.make_async_copy(src, dst, loc_sem.at[n]) for n, (src, dst) in enumerate(kv_parts(c))
    ]
    local.append(pltpu.make_async_copy(w_ref, wbuf.at[x * 2 + c], loc_sem.at[6]))
    local.append(pltpu.make_async_copy(q_ref, qbuf.at[me_block], loc_sem.at[7]))
    for copy in local:
        copy.start()

    barrier = pltpu.get_barrier_semaphore()

    def greet(dev):
        pl.semaphore_signal(barrier, inc=1, device_id=dev, device_id_type=MESH)

    def peer(n):
        return (seq_of((yl + n % 2) % 2, (x + n // 2) % 4), h)

    for n in range(1, 8):
        greet(peer(n))
    greet(partner)
    for d in (1, 2, 6, 7):
        greet((s, yh * 8 + (z + d) % 8))
    for a in range(2):
        greet((seq_of(a, x), yl * 8 + (z + 4) % 8))
    for a in range(2):
        @pl.when(jnp.logical_or(yl != yh, yl != a))
        def _():
            greet((seq_of(a, x), yl * 8 + z))

    pl.semaphore_wait(barrier, jnp.where(yl == yh, 15, 16))

    kv_out = [
        remote(src, dst, kv_send.at[n], kv_recv.at[n], partner)
        for n, (src, dst) in enumerate(kv_parts(c))
    ]

    def q_copy(g, n):
        rows = pl.ds(pl.multiple_of(g * RG, RG), RG)
        return remote(
            q_ref.at[rows], qbuf.at[me_block, rows], q_send.at[g, n], q_recv.at[g, me_block], peer(n)
        )

    def q_start(g):
        for n in (1, 2, 6, 3, 7, 4, 5):
            q_copy(g, n).start()

    q_start(0)
    for copy in kv_out:
        copy.start()

    my_w = x * 2 + c

    def w_rows(j):
        return pl.ds(pl.multiple_of(j * 128, 128), 128)

    def w_copy(d, j):
        return remote(
            w_ref.at[w_rows(j)], wbuf.at[my_w, w_rows(j)], w_send.at[d, j], w_recv.at[my_w, j],
            (seq_of(yl, (x + d) % 4), h),
        )

    def w_start(j):
        w_copy(1, j).start()
        w_copy(3, j).start()

    def w_on(j):
        step = 1 + 2 * (j % 2)
        slot = ((x + 4 - step) % 4) * 2 + c
        ref = wbuf.at[slot, w_rows(j)]
        return remote(
            ref, ref, w_send.at[2, j], w_recv.at[slot, j], (seq_of(yl, (x + step) % 4), h)
        )

    def w_forward(d):
        return remote(w_ref, wbuf.at[my_w], wf_send.at[0, 0], w_recv.at[my_w, 0], partner)

    def w_pass(d, j):
        slot = ((x + 4 - d) % 4) * 2 + c
        ref = wbuf.at[slot, w_rows(j)]
        return remote(ref, ref, wf_send.at[d, j], w_recv.at[slot, j], partner)

    def w_far(d, j):
        slot = ((x + 4 - d) % 4) * 2 + c
        arrived(wbuf.at[slot, w_rows(j)], w_recv.at[slot, j])

    def w_hand_on(j, last=False):
        w_far(1, j)
        w_far(3, j)
        if not last:
            w_on(j).start()
        w_pass(1, j).start()
        w_pass(3, j).start()

    def w_hand_far(j):
        w_far(2, j)
        w_pass(2, j).start()

    def w_partner(j):
        for d in (1, 3, 2):
            slot = ((x + 4 - d) % 4) * 2 + 1 - c
            arrived(wbuf.at[slot, w_rows(j)], w_recv.at[slot, j])

    def flip(rows):
        vt[pl.ds(0, HD), rows] = vraw[rows, :].T

    def flip_cached(core):
        def one(t, unused):
            flip(pl.ds(pl.multiple_of(core * SHARD + t * TK, TK), TK))
            return unused

        lax.fori_loop(0, SHARD // TK, one, 0)

    vt[pl.ds(HD, VR - HD), :] = jnp.ones((VR - HD, KEYS), BF16)
    for copy in local:
        copy.wait()
    flip_cached(c)

    def o_place(i, n):
        return (yl + n // 2) % 2, (x + 2 * (i % 2) + n % 2) % 4

    def o_copy(i, n):
        p, q = o_place(i, n)
        return remote(
            osend.at[i, n], obuf.at[i // 2, me_block], o_send.at[i, n], o_recv.at[i // 2, me_block],
            (seq_of(p, q), h),
        )

    def stage_o(i):
        for n in (2, 1, 3):
            o_copy(i, n).start()

        @pl.when(i % 2 == 0)
        def _():
            pltpu.make_async_copy(
                osend.at[i, 0], obuf.at[i // 2, me_block], o_recv.at[i // 2, me_block]
            ).start()

        @pl.when(i % 2 == 1)
        def _():
            o_copy(i, 0).start()

    def zz(d):
        return (z + 8 + d) % 8

    def m_copy(g, a, far):
        return remote(
            amine.at[g], abuf.at[z, g, yl], m_send.at[g, a, far], m_recv.at[g, far, yl],
            (seq_of(yh, x), a * 8 + zz(4 * far)),
        )

    def m_is_self(a):
        return jnp.logical_and(yl == yh, yh == a)

    def stage_m(g):
        for j in range(8):
            arrived(obuf.at[g, j], o_recv.at[g, j])
        result = merge([obuf[g, j] for j in range(8)])
        turned = result.T.astype(BF16)
        for n in range(G):
            amine[g, :, pl.ds(n * HD, HD)] = turned[n * RG : (n + 1) * RG]
        for a in range(2):
            m_copy(g, a, 1).start()
        for a in range(2):
            @pl.when(m_is_self(a))
            def _():
                pltpu.make_async_copy(amine.at[g], abuf.at[z, g, yl], m_recv.at[g, 0, yl]).start()

            @pl.when(jnp.logical_not(m_is_self(a)))
            def _():
                m_copy(g, a, 0).start()

    def z_copies(g):
        near, far = abuf.at[z, g], abuf.at[zz(4), g]
        plan = ((near, 2), (near, -2), (far, 1), (far, -1), (near, 1), (near, -1))
        return [
            remote(ref, ref, z_send.at[g, n], z_recv.at[g, n], (s, yh * 8 + zz(d)))
            for n, (ref, d) in enumerate(plan)
        ]

    def stage_z(g):
        for a in range(2):
            arrived(abuf.at[z, g, a], m_recv.at[g, 0, a])
            arrived(abuf.at[zz(4), g, a], m_recv.at[g, 1, a])
        copies = z_copies(g)
        for n in (4, 5, 0, 1, 2, 3):
            copies[n].start()

    def z_take(g, n):
        d = (-2, 2, 3, -3, -1, 1)[n]
        arrived(abuf.at[zz(d), g], z_recv.at[g, n])

    def z_wait(g):
        for n in range(6):
            z_take(g, n)

    def one_item(i, unused):
        g, sub = i // 2, i % 2
        places = [((yl + dy) % 2, (x + 2 * sub + k) % 4) for dy in range(2) for k in range(2)]

        @pl.when(jnp.logical_and(sub == 0, g < CH - 1))
        def _():
            q_start(g + 1)

        rows = pl.ds(pl.multiple_of(g * RG, RG), RG)
        for n, (a, b) in enumerate(places):
            block = a * 4 + b
            if n == 0:
                @pl.when(sub > 0)
                def _():
                    arrived(qbuf.at[block, rows], q_recv.at[g, block])
            else:
                arrived(qbuf.at[block, rows], q_recv.at[g, block])
        tall = jnp.concatenate(
            [qbuf[a * 4 + b, rows, pl.ds(n * HD, HD)] for a, b in places for n in range(G)], axis=0
        )
        qt[...] = tall.T

        def score(rows):
            return jnp.dot(keys[rows, :], qt[...], preferred_element_type=F32) * SCALE

        def highest(top, scores):
            return jnp.maximum(top, jnp.max(scores.reshape(TK // 8, 8, COLS), axis=0))

        top = jnp.full((8, COLS), -1e30, F32)
        for core in (c, 1 - c):
            for t in range(SHARD // TK):
                rows = pl.ds(pl.multiple_of(core * SHARD + t * TK, TK), TK)
                scores = score(rows)
                sbuf[rows, :] = scores
                top = highest(top, scores)
            if core is c:
                @pl.when(i == 0)
                def _():
                    for copy in kv_out[:2]:
                        copy.wait_recv()

        col = lax.broadcasted_iota(jnp.int32, (1, COLS), 1)
        base = jnp.zeros((1, COLS), jnp.int32)
        for n, (a, b) in enumerate(places):
            base = jnp.where(col // HD == n, seq_of(a, b) * 128, base)
        query_pos = base + g * RG + col % RG
        rows = pl.ds(CACHED, TK)
        key_pos = (yl * 8 + x * 2) * 128 + lax.broadcasted_iota(jnp.int32, (TK, COLS), 0)
        scores = jnp.where(key_pos <= query_pos, score(rows), -1e30)
        sbuf[rows, :] = scores
        top = jnp.max(highest(top, scores), axis=0, keepdims=True)

        @pl.when(i == 0)
        def _():
            for copy in kv_out[2:]:
                copy.wait_recv()
            flip_cached(1 - c)
            flip(pl.ds(CACHED, 256))

        @pl.when(jnp.logical_and(sub == 1, i >= 3))
        def _():
            stage_m((i - 3) // 2)

        summed = jnp.zeros((VR, COLS), F32)
        for t in range(KEYS // TK):
            weights = jnp.exp2(sbuf[pl.ds(t * TK, TK), :] - top).astype(BF16)
            summed = summed + jnp.dot(vt[:, pl.ds(t * TK, TK)], weights, preferred_element_type=F32)
        total = summed[HD : HD + 1]
        packed = message(summed[:HD] / total, top, total)
        for n in range(4):
            osend[i, n] = packed[:, n * HD : (n + 1) * HD]
        stage_o(i)

        @pl.when(jnp.logical_and(sub == 0, i >= 4))
        def _():
            stage_z((i - 4) // 2)

        @pl.when(i == 0)
        def _():
            w_forward(0).start()

        @pl.when(jnp.logical_and(sub == 0, i < 6))
        def _():
            w_start(i // 2)

        @pl.when(jnp.logical_and(sub == 1, i >= 3))
        def _():
            w_hand_on((i - 3) // 2)

        @pl.when(jnp.logical_and(sub == 1, i >= 5))
        def _():
            w_hand_far((i - 5) // 2)

        return unused

    lax.fori_loop(0, 2 * CH, one_item, 0)

    def multiply(first, count, place, low, high):
        rows = 2 * RG * count
        block = abuf[place, first : first + count].reshape(rows, 512)
        product = jnp.dot(
            block[:, low:high], wbuf[place, pl.ds(low, high - low), :], preferred_element_type=F32
        )
        acc[first : first + count] += product.reshape(count, 2, RG, 512)

    stage_m(CH - 1)
    w_start(3)
    w_copy(2, 3).start()
    stage_z(CH - 2)
    w_hand_far(2)
    acc[...] = jnp.zeros_like(acc)

    def drain_item(i, unused):
        for n in range(1, 4):
            o_copy(i, n).wait_send()

        @pl.when(i % 2 == 1)
        def _():
            o_copy(i, 0).wait_send()

        return unused

    lax.fori_loop(0, 2 * CH, drain_item, 0)
    for g in range(CH - 2):
        z_wait(g)
    slot = my_w + 1 - 2 * c
    arrived(wbuf.at[slot], w_recv.at[slot, 0])
    for j in range(3):
        w_partner(j)

    def first_part(place, unused):
        multiply(0, CH - 2, place, 0, 384)
        return unused

    lax.fori_loop(0, 8, first_part, 0)
    stage_z(CH - 1)
    w_hand_on(3, last=True)
    w_hand_far(3)

    def drain_chunk(g, unused):
        for n in range(1, 8):
            q_copy(g, n).wait_send()
        for a in range(2):
            m_copy(g, a, 1).wait_send()

            @pl.when(jnp.logical_not(m_is_self(a)))
            def _():
                m_copy(g, a, 0).wait_send()

        return unused

    lax.fori_loop(0, CH, drain_chunk, 0)
    z_wait(CH - 2)
    w_partner(3)

    def second_part(place, unused):
        multiply(0, CH - 2, place, 384, 512)
        multiply(CH - 2, 1, place, 0, 512)
        return unused

    lax.fori_loop(0, 8, second_part, 0)
    for g in range(CH - 1):
        csend[g] = acc[g, 1 - yl].astype(BF16)

    def swap(n):
        some = pl.ds(0, CH - 1) if n == 0 else pl.ds(CH - 1, 1)
        return remote(csend.at[some], cbuf.at[some], c_send.at[n], c_recv.at[n], y_mate)

    swap(0).start()

    for copy in kv_out:
        copy.wait_send()
    w_forward(0).wait_send()
    for j in range(4):
        for d in range(1, 4):
            if d == 2 and j < 3:
                w_on(j).wait_send()
            else:
                w_copy(d, j).wait_send()
            w_pass(d, j).wait_send()
    for g in range(CH - 1):
        for copy in z_copies(g):
            copy.wait_send()

    def last_part(place, unused):
        multiply(CH - 1, 1, place, 0, 512)
        return unused

    last_part(z, 0)
    last_part(zz(4), 0)
    for n, d in ((4, -1), (5, 1), (0, -2), (1, 2), (2, 3), (3, -3)):
        z_take(CH - 1, n)
        last_part(zz(d), 0)
    csend[CH - 1] = acc[CH - 1, 1 - yl].astype(BF16)
    swap(1).start()
    for copy in z_copies(CH - 1):
        copy.wait_send()
    swap(0).wait_recv()
    for g in range(CH):
        if g == CH - 1:
            swap(1).wait_recv()
        out_ref[pl.ds(g * RG, RG), :] = (acc[g, yl] + cbuf[g].astype(F32)).astype(BF16)

    for n in range(2):
        swap(n).wait_send()


def local(queries, cache_keys, cache_values, new_keys, new_values, out_weight):
    dma = pltpu.SemaphoreType.DMA
    hbm = pl.BlockSpec(memory_space=pltpu.HBM)
    vmem = pl.BlockSpec(memory_space=pltpu.VMEM)
    items = 2 * CH
    return pl.pallas_call(
        kernel,
        out_shape=jax.ShapeDtypeStruct((128, 512), BF16),
        in_specs=[vmem, hbm, hbm, hbm, hbm, hbm],
        out_specs=vmem,
        scratch_shapes=[
            pltpu.VMEM((KEYS, HD), BF16),
            pltpu.VMEM((KEYS, HD), BF16),
            pltpu.VMEM((VR, KEYS), BF16),
            pltpu.VMEM((KEYS, COLS), F32),
            pltpu.VMEM((8, 128, 512), BF16),
            pltpu.VMEM((HD, COLS), BF16),
            pltpu.VMEM((items, 4, VR, HD), BF16),
            pltpu.VMEM((CH, 8, VR, HD), BF16),
            pltpu.VMEM((CH, RG, 512), BF16),
            pltpu.VMEM((8, CH, 2, RG, 512), BF16),
            pltpu.VMEM((8, 512, 512), BF16),
            pltpu.VMEM((CH, 2, RG, 512), F32),
            pltpu.VMEM((CH, RG, 512), BF16),
            pltpu.VMEM((CH, RG, 512), BF16),
            dma((8,)), dma((4,)), dma((4,)), dma((CH, 8)), dma((CH, 8)),
            dma((4, 4)), dma((8, 4)), dma((4, 4)),
            dma((items, 4)), dma((CH, 8)),
            dma((CH, 2, 2)), dma((CH, 2, 2)), dma((CH, 6)), dma((CH, 6)),
            dma((2,)), dma((2,)),
        ],
        compiler_params=pltpu.CompilerParams(
            collective_id=0, has_side_effects=True, vmem_limit_bytes=60 * 2**20
        ),
        cost_estimate=pl.CostEstimate(
            flops=11_000_000_000, bytes_accessed=4_000_000, transcendentals=18_000_000
        ),
    )(queries, cache_keys, cache_values, new_keys, new_values, out_weight)


def solution(mesh):
    placed = (
        P("seq", "head"),
        P("seq", None),
        P("seq", None),
        P("seq", None),
        P("seq", None),
        P("seq", "head"),
    )
    return jax.shard_map(
        local, mesh=mesh, in_specs=placed, out_specs=P("seq", "head"), check_vma=False
    )
```

```python
import functools

import jax
import jax.numpy as jnp
import numpy as np
from jax import lax
from jax.experimental import pallas as pl
from jax.experimental.pallas import tpu as pltpu
from jax.sharding import PartitionSpec as P

HD = 128
G = 4
CH = 4
RG = 128 // CH
COLS = 512
SHARD = 2048
CACHED = 2 * SHARD
KEYS = CACHED + 256
TK = 256
VR = 144
SCALE = float(HD**-0.5 * np.log2(np.e))
MESH = pl.DeviceIdType.MESH
F32, BF16 = jnp.float32, jnp.bfloat16


def pieces(row):
    a = row.astype(BF16).astype(F32)
    b = (row - a).astype(BF16).astype(F32)
    return [a, b, row - a - b]


def message(result, top, total):
    zeros = jnp.zeros((10, result.shape[1]), F32)
    tail = jnp.concatenate(pieces(top) + pieces(total) + [zeros], axis=0)
    return jnp.concatenate([result.astype(BF16), tail.astype(BF16)], axis=0)


def merge(messages):
    tops, totals = [], []
    for one in messages:
        tail = one[HD:].astype(F32)
        tops.append(tail[0:1] + tail[1:2] + tail[2:3])
        totals.append(tail[3:4] + tail[4:5] + tail[5:6])
    top = functools.reduce(jnp.maximum, tops)
    parts = [b * jnp.exp2(a - top) for a, b in zip(tops, totals)]
    total = functools.reduce(jnp.add, parts)
    result = functools.reduce(
        jnp.add, [one[:HD].astype(F32) * (part / total) for one, part in zip(messages, parts)]
    )
    return result


def kernel(
    q_ref, ck_ref, cv_ref, nk_ref, nv_ref, w_ref, out_ref,
    keys, vraw, vt, sbuf, qbuf, qt, osend, obuf, amine, abuf, wbuf, acc, csend, cbuf,
    loc_sem, kv_send, kv_recv, q_send, q_recv, w_send, w_recv, wf_send,
    o_send, o_recv, m_send, m_recv, z_send, z_recv, c_send, c_recv,
):
    s = lax.axis_index("seq")
    h = lax.axis_index("head")
    yl, x, c = s // 8, (s // 2) % 4, s % 2
    yh, z = h // 8, h % 8
    me_block = yl * 4 + x
    partner = (s + 1 - 2 * c, h)

    def seq_of(a, b):
        return a * 8 + b * 2 + c

    y_mate = (seq_of(1 - yl, x), h)

    def remote(src, dst, ssem, rsem, dev):
        return pltpu.make_async_remote_copy(
            src_ref=src, dst_ref=dst, send_sem=ssem, recv_sem=rsem, device_id=dev, device_id_type=MESH
        )

    def arrived(ref, sem):
        pltpu.make_async_copy(ref, ref, sem).wait()

    kv_col = pl.ds(pl.multiple_of((h // 2) * HD, HD), HD)

    def cached_rows(core):
        return pl.ds(pl.multiple_of(core * SHARD, SHARD), SHARD)

    def new_rows(core):
        return pl.ds(pl.multiple_of(CACHED + core * 128, 128), 128)

    def kv_parts(core):
        return [
            (ck_ref.at[:, kv_col], keys.at[cached_rows(core), :]),
            (nk_ref.at[:, kv_col], keys.at[new_rows(core), :]),
            (cv_ref.at[:, kv_col], vraw.at[cached_rows(core), :]),
            (nv_ref.at[:, kv_col], vraw.at[new_rows(core), :]),
        ]

    local = [
        pltpu.make_async_copy(src, dst, loc_sem.at[n]) for n, (src, dst) in enumerate(kv_parts(c))
    ]
    local.append(pltpu.make_async_copy(w_ref, wbuf.at[x * 2 + c], loc_sem.at[6]))
    local.append(pltpu.make_async_copy(q_ref, qbuf.at[me_block], loc_sem.at[7]))
    for copy in local:
        copy.start()

    barrier = pltpu.get_barrier_semaphore()

    def greet(dev):
        pl.semaphore_signal(barrier, inc=1, device_id=dev, device_id_type=MESH)

    def peer(n):
        return (seq_of((yl + n % 2) % 2, (x + n // 2) % 4), h)

    for n in range(1, 8):
        greet(peer(n))
    greet(partner)
    for d in (1, 2, 6, 7):
        greet((s, yh * 8 + (z + d) % 8))
    for a in range(2):
        greet((seq_of(a, x), yl * 8 + (z + 4) % 8))
    for a in range(2):
        @pl.when(jnp.logical_or(yl != yh, yl != a))
        def _():
            greet((seq_of(a, x), yl * 8 + z))

    pl.semaphore_wait(barrier, jnp.where(yl == yh, 15, 16))

    kv_out = [
        remote(src, dst, kv_send.at[n], kv_recv.at[n], partner)
        for n, (src, dst) in enumerate(kv_parts(c))
    ]

    def q_copy(g, n):
        rows = pl.ds(pl.multiple_of(g * RG, RG), RG)
        return remote(
            q_ref.at[rows], qbuf.at[me_block, rows], q_send.at[g, n], q_recv.at[g, me_block], peer(n)
        )

    def q_start(g):
        for n in (1, 2, 6, 3, 7, 4, 5):
            q_copy(g, n).start()

    q_start(0)
    for copy in kv_out:
        copy.start()

    my_w = x * 2 + c

    def w_rows(j):
        return pl.ds(pl.multiple_of(j * 128, 128), 128)

    def w_copy(d, j):
        return remote(
            w_ref.at[w_rows(j)], wbuf.at[my_w, w_rows(j)], w_send.at[d, j], w_recv.at[my_w, j],
            (seq_of(yl, (x + d) % 4), h),
        )

    def w_start(j):
        w_copy(1, j).start()
        w_copy(3, j).start()

    def w_on(j):
        step = 1 + 2 * (j % 2)
        slot = ((x + 4 - step) % 4) * 2 + c
        ref = wbuf.at[slot, w_rows(j)]
        return remote(
            ref, ref, w_send.at[2, j], w_recv.at[slot, j], (seq_of(yl, (x + step) % 4), h)
        )

    def w_forward(d):
        return remote(w_ref, wbuf.at[my_w], wf_send.at[0, 0], w_recv.at[my_w, 0], partner)

    def w_pass(d, j):
        slot = ((x + 4 - d) % 4) * 2 + c
        ref = wbuf.at[slot, w_rows(j)]
        return remote(ref, ref, wf_send.at[d, j], w_recv.at[slot, j], partner)

    def w_far(d, j):
        slot = ((x + 4 - d) % 4) * 2 + c
        arrived(wbuf.at[slot, w_rows(j)], w_recv.at[slot, j])

    def w_hand_on(j, last=False):
        w_far(1, j)
        w_far(3, j)
        if not last:
            w_on(j).start()
        w_pass(1, j).start()
        w_pass(3, j).start()

    def w_hand_far(j):
        w_far(2, j)
        w_pass(2, j).start()

    def w_partner(j):
        for d in (1, 3, 2):
            slot = ((x + 4 - d) % 4) * 2 + 1 - c
            arrived(wbuf.at[slot, w_rows(j)], w_recv.at[slot, j])

    def flip(rows):
        vt[pl.ds(0, HD), rows] = vraw[rows, :].T

    def flip_cached(core):
        def one(t, unused):
            flip(pl.ds(pl.multiple_of(core * SHARD + t * TK, TK), TK))
            return unused

        lax.fori_loop(0, SHARD // TK, one, 0)

    vt[pl.ds(HD, VR - HD), :] = jnp.ones((VR - HD, KEYS), BF16)
    for copy in local:
        copy.wait()
    flip_cached(c)

    def o_place(i, n):
        return (yl + n // 2) % 2, (x + 2 * (i % 2) + n % 2) % 4

    def o_copy(i, n):
        p, q = o_place(i, n)
        return remote(
            osend.at[i, n], obuf.at[i // 2, me_block], o_send.at[i, n], o_recv.at[i // 2, me_block],
            (seq_of(p, q), h),
        )

    def stage_o(i):
        for n in (2, 1, 3):
            o_copy(i, n).start()

        @pl.when(i % 2 == 0)
        def _():
            pltpu.make_async_copy(
                osend.at[i, 0], obuf.at[i // 2, me_block], o_recv.at[i // 2, me_block]
            ).start()

        @pl.when(i % 2 == 1)
        def _():
            o_copy(i, 0).start()

    def zz(d):
        return (z + 8 + d) % 8

    def m_copy(g, a, far):
        return remote(
            amine.at[g], abuf.at[z, g, yl], m_send.at[g, a, far], m_recv.at[g, far, yl],
            (seq_of(yh, x), a * 8 + zz(4 * far)),
        )

    def m_is_self(a):
        return jnp.logical_and(yl == yh, yh == a)

    def stage_m(g):
        for j in range(8):
            arrived(obuf.at[g, j], o_recv.at[g, j])
        result = merge([obuf[g, j] for j in range(8)])
        turned = result.T.astype(BF16)
        for n in range(G):
            amine[g, :, pl.ds(n * HD, HD)] = turned[n * RG : (n + 1) * RG]
        for a in range(2):
            m_copy(g, a, 1).start()
        for a in range(2):
            @pl.when(m_is_self(a))
            def _():
                pltpu.make_async_copy(amine.at[g], abuf.at[z, g, yl], m_recv.at[g, 0, yl]).start()

            @pl.when(jnp.logical_not(m_is_self(a)))
            def _():
                m_copy(g, a, 0).start()

    def z_copies(g):
        near, far = abuf.at[z, g], abuf.at[zz(4), g]
        plan = ((near, 2), (near, -2), (far, 1), (far, -1), (near, 1), (near, -1))
        return [
            remote(ref, ref, z_send.at[g, n], z_recv.at[g, n], (s, yh * 8 + zz(d)))
            for n, (ref, d) in enumerate(plan)
        ]

    def stage_z(g):
        for a in range(2):
            arrived(abuf.at[z, g, a], m_recv.at[g, 0, a])
            arrived(abuf.at[zz(4), g, a], m_recv.at[g, 1, a])
        copies = z_copies(g)
        for n in (4, 5, 0, 1, 2, 3):
            copies[n].start()

    def z_take(g, n):
        d = (-2, 2, 3, -3, -1, 1)[n]
        arrived(abuf.at[zz(d), g], z_recv.at[g, n])

    def z_wait(g):
        for n in range(6):
            z_take(g, n)

    def one_item(i, unused):
        g, sub = i // 2, i % 2
        places = [((yl + dy) % 2, (x + 2 * sub + k) % 4) for dy in range(2) for k in range(2)]

        @pl.when(jnp.logical_and(sub == 0, g < CH - 1))
        def _():
            q_start(g + 1)

        rows = pl.ds(pl.multiple_of(g * RG, RG), RG)
        for n, (a, b) in enumerate(places):
            block = a * 4 + b
            if n == 0:
                @pl.when(sub > 0)
                def _():
                    arrived(qbuf.at[block, rows], q_recv.at[g, block])
            else:
                arrived(qbuf.at[block, rows], q_recv.at[g, block])
        tall = jnp.concatenate(
            [qbuf[a * 4 + b, rows, pl.ds(n * HD, HD)] for a, b in places for n in range(G)], axis=0
        )
        qt[...] = tall.T

        def score(rows):
            return jnp.dot(keys[rows, :], qt[...], preferred_element_type=F32) * SCALE

        def highest(top, scores):
            return jnp.maximum(top, jnp.max(scores.reshape(TK // 8, 8, COLS), axis=0))

        top = jnp.full((8, COLS), -1e30, F32)
        for core in (c, 1 - c):
            for t in range(SHARD // TK):
                rows = pl.ds(pl.multiple_of(core * SHARD + t * TK, TK), TK)
                scores = score(rows)
                sbuf[rows, :] = scores
                top = highest(top, scores)
            if core is c:
                @pl.when(i == 0)
                def _():
                    for copy in kv_out[:2]:
                        copy.wait_recv()

        col = lax.broadcasted_iota(jnp.int32, (1, COLS), 1)
        base = jnp.zeros((1, COLS), jnp.int32)
        for n, (a, b) in enumerate(places):
            base = jnp.where(col // HD == n, seq_of(a, b) * 128, base)
        query_pos = base + g * RG + col % RG
        rows = pl.ds(CACHED, TK)
        key_pos = (yl * 8 + x * 2) * 128 + lax.broadcasted_iota(jnp.int32, (TK, COLS), 0)
        scores = jnp.where(key_pos <= query_pos, score(rows), -1e30)
        sbuf[rows, :] = scores
        top = jnp.max(highest(top, scores), axis=0, keepdims=True)

        @pl.when(i == 0)
        def _():
            for copy in kv_out[2:]:
                copy.wait_recv()
            flip_cached(1 - c)
            flip(pl.ds(CACHED, 256))

        @pl.when(jnp.logical_and(sub == 1, i >= 3))
        def _():
            stage_m((i - 3) // 2)

        summed = jnp.zeros((VR, COLS), F32)
        for t in range(KEYS // TK):
            weights = jnp.exp2(sbuf[pl.ds(t * TK, TK), :] - top).astype(BF16)
            summed = summed + jnp.dot(vt[:, pl.ds(t * TK, TK)], weights, preferred_element_type=F32)
        total = summed[HD : HD + 1]
        packed = message(summed[:HD] / total, top, total)
        for n in range(4):
            osend[i, n] = packed[:, n * HD : (n + 1) * HD]
        stage_o(i)

        @pl.when(jnp.logical_and(sub == 0, i >= 4))
        def _():
            stage_z((i - 4) // 2)

        @pl.when(i == 0)
        def _():
            w_forward(0).start()

        @pl.when(jnp.logical_and(sub == 0, i < 6))
        def _():
            w_start(i // 2)

        @pl.when(jnp.logical_and(sub == 1, i >= 3))
        def _():
            w_hand_on((i - 3) // 2)

        @pl.when(jnp.logical_and(sub == 1, i >= 5))
        def _():
            w_hand_far((i - 5) // 2)

        return unused

    lax.fori_loop(0, 2 * CH, one_item, 0)

    def multiply(first, count, place, low, high):
        rows = 2 * RG * count
        block = abuf[place, first : first + count].reshape(rows, 512)
        product = jnp.dot(
            block[:, low:high], wbuf[place, pl.ds(low, high - low), :], preferred_element_type=F32
        )
        acc[first : first + count] += product.reshape(count, 2, RG, 512)

    stage_m(CH - 1)
    w_start(3)
    w_copy(2, 3).start()
    stage_z(CH - 2)
    w_hand_far(2)
    acc[...] = jnp.zeros_like(acc)

    def drain_item(i, unused):
        for n in range(1, 4):
            o_copy(i, n).wait_send()

        @pl.when(i % 2 == 1)
        def _():
            o_copy(i, 0).wait_send()

        return unused

    lax.fori_loop(0, 2 * CH, drain_item, 0)
    def first_part(place, unused):
        multiply(0, CH - 2, place, 0, 384)
        return unused

    stage_z(CH - 1)
    for g in range(CH - 2):
        z_wait(g)
    slot = my_w + 1 - 2 * c
    arrived(wbuf.at[slot], w_recv.at[slot, 0])
    for j in range(3):
        w_partner(j)
    lax.fori_loop(0, 8, first_part, 0)
    w_hand_on(3, last=True)
    w_hand_far(3)

    def drain_chunk(g, unused):
        for n in range(1, 8):
            q_copy(g, n).wait_send()
        for a in range(2):
            m_copy(g, a, 1).wait_send()

            @pl.when(jnp.logical_not(m_is_self(a)))
            def _():
                m_copy(g, a, 0).wait_send()

        return unused

    lax.fori_loop(0, CH, drain_chunk, 0)
    z_wait(CH - 2)
    w_partner(3)

    def second_part(place, unused):
        multiply(0, CH - 2, place, 384, 512)
        multiply(CH - 2, 1, place, 0, 512)
        return unused

    lax.fori_loop(0, 8, second_part, 0)
    for g in range(CH - 1):
        csend[g] = acc[g, 1 - yl].astype(BF16)

    def swap(n):
        some = pl.ds(0, CH - 1) if n == 0 else pl.ds(CH - 1, 1)
        return remote(csend.at[some], cbuf.at[some], c_send.at[n], c_recv.at[n], y_mate)

    swap(0).start()

    def last_part(place, unused):
        multiply(CH - 1, 1, place, 0, 512)
        return unused

    last_part(z, 0)
    last_part(zz(4), 0)
    for n, d in ((4, -1), (5, 1), (0, -2), (1, 2), (2, 3), (3, -3)):
        z_take(CH - 1, n)
        last_part(zz(d), 0)
    csend[CH - 1] = acc[CH - 1, 1 - yl].astype(BF16)
    swap(1).start()
    for copy in kv_out:
        copy.wait_send()
    w_forward(0).wait_send()
    for j in range(4):
        for d in range(1, 4):
            if d == 2 and j < 3:
                w_on(j).wait_send()
            else:
                w_copy(d, j).wait_send()
            w_pass(d, j).wait_send()
    for g in range(CH - 1):
        for copy in z_copies(g):
            copy.wait_send()
    for copy in z_copies(CH - 1):
        copy.wait_send()
    swap(0).wait_recv()
    for g in range(CH):
        if g == CH - 1:
            swap(1).wait_recv()
        out_ref[pl.ds(g * RG, RG), :] = (acc[g, yl] + cbuf[g].astype(F32)).astype(BF16)

    for n in range(2):
        swap(n).wait_send()


def local(queries, cache_keys, cache_values, new_keys, new_values, out_weight):
    dma = pltpu.SemaphoreType.DMA
    hbm = pl.BlockSpec(memory_space=pltpu.HBM)
    vmem = pl.BlockSpec(memory_space=pltpu.VMEM)
    items = 2 * CH
    return pl.pallas_call(
        kernel,
        out_shape=jax.ShapeDtypeStruct((128, 512), BF16),
        in_specs=[vmem, hbm, hbm, hbm, hbm, hbm],
        out_specs=vmem,
        scratch_shapes=[
            pltpu.VMEM((KEYS, HD), BF16),
            pltpu.VMEM((KEYS, HD), BF16),
            pltpu.VMEM((VR, KEYS), BF16),
            pltpu.VMEM((KEYS, COLS), F32),
            pltpu.VMEM((8, 128, 512), BF16),
            pltpu.VMEM((HD, COLS), BF16),
            pltpu.VMEM((items, 4, VR, HD), BF16),
            pltpu.VMEM((CH, 8, VR, HD), BF16),
            pltpu.VMEM((CH, RG, 512), BF16),
            pltpu.VMEM((8, CH, 2, RG, 512), BF16),
            pltpu.VMEM((8, 512, 512), BF16),
            pltpu.VMEM((CH, 2, RG, 512), F32),
            pltpu.VMEM((CH, RG, 512), BF16),
            pltpu.VMEM((CH, RG, 512), BF16),
            dma((8,)), dma((4,)), dma((4,)), dma((CH, 8)), dma((CH, 8)),
            dma((4, 4)), dma((8, 4)), dma((4, 4)),
            dma((items, 4)), dma((CH, 8)),
            dma((CH, 2, 2)), dma((CH, 2, 2)), dma((CH, 6)), dma((CH, 6)),
            dma((2,)), dma((2,)),
        ],
        compiler_params=pltpu.CompilerParams(
            collective_id=0, has_side_effects=True, vmem_limit_bytes=60 * 2**20
        ),
        cost_estimate=pl.CostEstimate(
            flops=11_000_000_000, bytes_accessed=4_000_000, transcendentals=18_000_000
        ),
    )(queries, cache_keys, cache_values, new_keys, new_values, out_weight)


def solution(mesh):
    placed = (
        P("seq", "head"),
        P("seq", None),
        P("seq", None),
        P("seq", None),
        P("seq", None),
        P("seq", "head"),
    )
    return jax.shard_map(
        local, mesh=mesh, in_specs=placed, out_specs=P("seq", "head"), check_vma=False
    )
```

```python
import functools

import jax
import jax.numpy as jnp
import numpy as np
from jax import lax
from jax.experimental import pallas as pl
from jax.experimental.pallas import tpu as pltpu
from jax.sharding import PartitionSpec as P

HD = 128
G = 4
CH = 4
RG = 128 // CH
COLS = 512
SHARD = 2048
CACHED = 2 * SHARD
KEYS = CACHED + 256
TK = 256
VR = 144
SCALE = float(HD**-0.5 * np.log2(np.e))
MESH = pl.DeviceIdType.MESH
F32, BF16 = jnp.float32, jnp.bfloat16


def pieces(row):
    a = row.astype(BF16).astype(F32)
    b = (row - a).astype(BF16).astype(F32)
    return [a, b, row - a - b]


def message(result, top, total):
    zeros = jnp.zeros((10, result.shape[1]), F32)
    tail = jnp.concatenate(pieces(top) + pieces(total) + [zeros], axis=0)
    return jnp.concatenate([result.astype(BF16), tail.astype(BF16)], axis=0)


def merge(messages):
    tops, totals = [], []
    for one in messages:
        tail = one[HD:].astype(F32)
        tops.append(tail[0:1] + tail[1:2] + tail[2:3])
        totals.append(tail[3:4] + tail[4:5] + tail[5:6])
    top = functools.reduce(jnp.maximum, tops)
    parts = [b * jnp.exp2(a - top) for a, b in zip(tops, totals)]
    total = functools.reduce(jnp.add, parts)
    result = functools.reduce(
        jnp.add, [one[:HD].astype(F32) * (part / total) for one, part in zip(messages, parts)]
    )
    return result


def kernel(
    q_ref, ck_ref, cv_ref, nk_ref, nv_ref, w_ref, out_ref,
    keys, vraw, vt, sbuf, qbuf, qt, osend, obuf, amine, abuf, wbuf, acc, csend, cbuf,
    loc_sem, kv_send, kv_recv, q_send, q_recv, w_send, w_recv, wf_send,
    o_send, o_recv, m_send, m_recv, z_send, z_recv, c_send, c_recv,
):
    s = lax.axis_index("seq")
    h = lax.axis_index("head")
    yl, x, c = s // 8, (s // 2) % 4, s % 2
    yh, z = h // 8, h % 8
    me_block = yl * 4 + x
    partner = (s + 1 - 2 * c, h)

    def seq_of(a, b):
        return a * 8 + b * 2 + c

    y_mate = (seq_of(1 - yl, x), h)

    def remote(src, dst, ssem, rsem, dev):
        return pltpu.make_async_remote_copy(
            src_ref=src, dst_ref=dst, send_sem=ssem, recv_sem=rsem, device_id=dev, device_id_type=MESH
        )

    def arrived(ref, sem):
        pltpu.make_async_copy(ref, ref, sem).wait()

    kv_col = pl.ds(pl.multiple_of((h // 2) * HD, HD), HD)

    def cached_rows(core):
        return pl.ds(pl.multiple_of(core * SHARD, SHARD), SHARD)

    def new_rows(core):
        return pl.ds(pl.multiple_of(CACHED + core * 128, 128), 128)

    def kv_parts(core):
        return [
            (ck_ref.at[:, kv_col], keys.at[cached_rows(core), :]),
            (nk_ref.at[:, kv_col], keys.at[new_rows(core), :]),
            (cv_ref.at[:, kv_col], vraw.at[cached_rows(core), :]),
            (nv_ref.at[:, kv_col], vraw.at[new_rows(core), :]),
        ]

    local = [
        pltpu.make_async_copy(src, dst, loc_sem.at[n]) for n, (src, dst) in enumerate(kv_parts(c))
    ]
    local.append(pltpu.make_async_copy(w_ref, wbuf.at[x * 2 + c], loc_sem.at[6]))
    local.append(pltpu.make_async_copy(q_ref, qbuf.at[me_block], loc_sem.at[7]))
    for copy in local:
        copy.start()

    barrier = pltpu.get_barrier_semaphore()

    def greet(dev):
        pl.semaphore_signal(barrier, inc=1, device_id=dev, device_id_type=MESH)

    def peer(n):
        return (seq_of((yl + n % 2) % 2, (x + n // 2) % 4), h)

    for n in range(1, 8):
        greet(peer(n))
    greet(partner)
    for d in (1, 2, 6, 7):
        greet((s, yh * 8 + (z + d) % 8))
    for a in range(2):
        greet((seq_of(a, x), yl * 8 + (z + 4) % 8))
    for a in range(2):
        @pl.when(jnp.logical_or(yl != yh, yl != a))
        def _():
            greet((seq_of(a, x), yl * 8 + z))

    pl.semaphore_wait(barrier, jnp.where(yl == yh, 15, 16))

    kv_out = [
        remote(src, dst, kv_send.at[n], kv_recv.at[n], partner)
        for n, (src, dst) in enumerate(kv_parts(c))
    ]

    def q_copy(g, n):
        rows = pl.ds(pl.multiple_of(g * RG, RG), RG)
        return remote(
            q_ref.at[rows], qbuf.at[me_block, rows], q_send.at[g, n], q_recv.at[g, me_block], peer(n)
        )

    def q_start(g):
        for n in (1, 2, 6, 3, 7, 4, 5):
            q_copy(g, n).start()

    q_start(0)
    for copy in kv_out:
        copy.start()

    my_w = x * 2 + c

    def w_rows(j):
        return pl.ds(pl.multiple_of(j * 128, 128), 128)

    def w_copy(d, j):
        return remote(
            w_ref.at[w_rows(j)], wbuf.at[my_w, w_rows(j)], w_send.at[d, j], w_recv.at[my_w, j],
            (seq_of(yl, (x + d) % 4), h),
        )

    def w_start(j):
        w_copy(1, j).start()
        w_copy(3, j).start()

    def w_on(j):
        step = 1 + 2 * (j % 2)
        slot = ((x + 4 - step) % 4) * 2 + c
        ref = wbuf.at[slot, w_rows(j)]
        return remote(
            ref, ref, w_send.at[2, j], w_recv.at[slot, j], (seq_of(yl, (x + step) % 4), h)
        )

    def w_forward(d):
        return remote(w_ref, wbuf.at[my_w], wf_send.at[0, 0], w_recv.at[my_w, 0], partner)

    def w_pass(d, j):
        slot = ((x + 4 - d) % 4) * 2 + c
        ref = wbuf.at[slot, w_rows(j)]
        return remote(ref, ref, wf_send.at[d, j], w_recv.at[slot, j], partner)

    def w_far(d, j):
        slot = ((x + 4 - d) % 4) * 2 + c
        arrived(wbuf.at[slot, w_rows(j)], w_recv.at[slot, j])

    def w_hand_on(j, last=False):
        w_far(1, j)
        w_far(3, j)
        if not last:
            w_on(j).start()
        w_pass(1, j).start()
        w_pass(3, j).start()

    def w_hand_far(j):
        w_far(2, j)
        w_pass(2, j).start()

    def w_partner(j):
        for d in (1, 3, 2):
            slot = ((x + 4 - d) % 4) * 2 + 1 - c
            arrived(wbuf.at[slot, w_rows(j)], w_recv.at[slot, j])

    def flip(rows):
        vt[pl.ds(0, HD), rows] = vraw[rows, :].T

    def flip_cached(core):
        def one(t, unused):
            flip(pl.ds(pl.multiple_of(core * SHARD + t * TK, TK), TK))
            return unused

        lax.fori_loop(0, SHARD // TK, one, 0)

    vt[pl.ds(HD, VR - HD), :] = jnp.ones((VR - HD, KEYS), BF16)
    for copy in local:
        copy.wait()
    flip_cached(c)

    def o_place(i, n):
        return (yl + n // 2) % 2, (x + 2 * (i % 2) + n % 2) % 4

    def o_copy(i, n):
        p, q = o_place(i, n)
        return remote(
            osend.at[i, n], obuf.at[i // 2, me_block], o_send.at[i, n], o_recv.at[i // 2, me_block],
            (seq_of(p, q), h),
        )

    def stage_o(i):
        for n in (2, 1, 3):
            o_copy(i, n).start()

        @pl.when(i % 2 == 0)
        def _():
            pltpu.make_async_copy(
                osend.at[i, 0], obuf.at[i // 2, me_block], o_recv.at[i // 2, me_block]
            ).start()

        @pl.when(i % 2 == 1)
        def _():
            o_copy(i, 0).start()

    def zz(d):
        return (z + 8 + d) % 8

    def m_copy(g, a, far):
        return remote(
            amine.at[g], abuf.at[z, g, yl], m_send.at[g, a, far], m_recv.at[g, far, yl],
            (seq_of(yh, x), a * 8 + zz(4 * far)),
        )

    def m_is_self(a):
        return jnp.logical_and(yl == yh, yh == a)

    def stage_m(g):
        for j in range(8):
            arrived(obuf.at[g, j], o_recv.at[g, j])
        result = merge([obuf[g, j] for j in range(8)])
        turned = result.T.astype(BF16)
        for n in range(G):
            amine[g, :, pl.ds(n * HD, HD)] = turned[n * RG : (n + 1) * RG]
        for a in range(2):
            m_copy(g, a, 1).start()
        for a in range(2):
            @pl.when(m_is_self(a))
            def _():
                pltpu.make_async_copy(amine.at[g], abuf.at[z, g, yl], m_recv.at[g, 0, yl]).start()

            @pl.when(jnp.logical_not(m_is_self(a)))
            def _():
                m_copy(g, a, 0).start()

    def z_copies(g):
        near, far = abuf.at[z, g], abuf.at[zz(4), g]
        plan = ((near, 2), (near, -2), (far, 1), (far, -1), (near, 1), (near, -1))
        return [
            remote(ref, ref, z_send.at[g, n], z_recv.at[g, n], (s, yh * 8 + zz(d)))
            for n, (ref, d) in enumerate(plan)
        ]

    def stage_z(g):
        for a in range(2):
            arrived(abuf.at[z, g, a], m_recv.at[g, 0, a])
            arrived(abuf.at[zz(4), g, a], m_recv.at[g, 1, a])
        copies = z_copies(g)
        for n in (4, 5, 0, 1, 2, 3):
            copies[n].start()

    def z_take(g, n):
        d = (-2, 2, 3, -3, -1, 1)[n]
        arrived(abuf.at[zz(d), g], z_recv.at[g, n])

    def z_wait(g):
        for n in range(6):
            z_take(g, n)

    def one_item(i, unused):
        g, sub = i // 2, i % 2
        places = [((yl + dy) % 2, (x + 2 * sub + k) % 4) for dy in range(2) for k in range(2)]

        @pl.when(jnp.logical_and(sub == 0, g < CH - 1))
        def _():
            q_start(g + 1)

        rows = pl.ds(pl.multiple_of(g * RG, RG), RG)
        for n, (a, b) in enumerate(places):
            block = a * 4 + b
            if n == 0:
                @pl.when(sub > 0)
                def _():
                    arrived(qbuf.at[block, rows], q_recv.at[g, block])
            else:
                arrived(qbuf.at[block, rows], q_recv.at[g, block])
        tall = jnp.concatenate(
            [qbuf[a * 4 + b, rows, pl.ds(n * HD, HD)] for a, b in places for n in range(G)], axis=0
        )
        qt[...] = tall.T

        def score(rows):
            return jnp.dot(keys[rows, :], qt[...], preferred_element_type=F32) * SCALE

        def highest(top, scores):
            return jnp.maximum(top, jnp.max(scores.reshape(TK // 8, 8, COLS), axis=0))

        top = jnp.full((8, COLS), -1e30, F32)
        for core in (c, 1 - c):
            for t in range(SHARD // TK):
                rows = pl.ds(pl.multiple_of(core * SHARD + t * TK, TK), TK)
                scores = score(rows)
                sbuf[rows, :] = scores
                top = highest(top, scores)
            if core is c:
                @pl.when(i == 0)
                def _():
                    for copy in kv_out[:2]:
                        copy.wait_recv()

        col = lax.broadcasted_iota(jnp.int32, (1, COLS), 1)
        base = jnp.zeros((1, COLS), jnp.int32)
        for n, (a, b) in enumerate(places):
            base = jnp.where(col // HD == n, seq_of(a, b) * 128, base)
        query_pos = base + g * RG + col % RG
        rows = pl.ds(CACHED, TK)
        key_pos = (yl * 8 + x * 2) * 128 + lax.broadcasted_iota(jnp.int32, (TK, COLS), 0)
        scores = jnp.where(key_pos <= query_pos, score(rows), -1e30)
        sbuf[rows, :] = scores
        top = jnp.max(highest(top, scores), axis=0, keepdims=True)

        @pl.when(i == 0)
        def _():
            for copy in kv_out[2:]:
                copy.wait_recv()
            flip_cached(1 - c)
            flip(pl.ds(CACHED, 256))

        @pl.when(jnp.logical_and(sub == 1, i >= 3))
        def _():
            stage_m((i - 3) // 2)

        summed = jnp.zeros((VR, COLS), F32)
        for t in range(KEYS // TK):
            weights = jnp.exp2(sbuf[pl.ds(t * TK, TK), :] - top).astype(BF16)
            summed = summed + jnp.dot(vt[:, pl.ds(t * TK, TK)], weights, preferred_element_type=F32)
        total = summed[HD : HD + 1]
        packed = message(summed[:HD] / total, top, total)
        for n in range(4):
            osend[i, n] = packed[:, n * HD : (n + 1) * HD]
        stage_o(i)

        @pl.when(jnp.logical_and(sub == 0, i >= 4))
        def _():
            stage_z((i - 4) // 2)

        @pl.when(i == 0)
        def _():
            w_forward(0).start()

        @pl.when(jnp.logical_and(sub == 0, i < 6))
        def _():
            w_start(i // 2)

        @pl.when(jnp.logical_and(sub == 1, i >= 3))
        def _():
            w_hand_on((i - 3) // 2)

        @pl.when(jnp.logical_and(sub == 1, i >= 5))
        def _():
            w_hand_far((i - 5) // 2)

        return unused

    lax.fori_loop(0, 2 * CH, one_item, 0)

    def multiply(first, count, place, low, high):
        rows = 2 * RG * count
        block = abuf[place, first : first + count].reshape(rows, 512)
        product = jnp.dot(
            block[:, low:high], wbuf[place, pl.ds(low, high - low), :], preferred_element_type=F32
        )
        acc[first : first + count] += product.reshape(count, 2, RG, 512)

    stage_m(CH - 1)
    w_start(3)
    w_copy(2, 3).start()
    stage_z(CH - 2)
    w_hand_far(2)
    acc[...] = jnp.zeros_like(acc)

    def drain_item(i, unused):
        for n in range(1, 4):
            o_copy(i, n).wait_send()

        @pl.when(i % 2 == 1)
        def _():
            o_copy(i, 0).wait_send()

        return unused

    lax.fori_loop(0, 2 * CH, drain_item, 0)
    for g in range(CH - 2):
        z_wait(g)
    slot = my_w + 1 - 2 * c
    arrived(wbuf.at[slot], w_recv.at[slot, 0])
    for j in range(3):
        w_partner(j)

    def first_part(place, unused):
        multiply(0, CH - 2, place, 0, 384)
        return unused

    lax.fori_loop(0, 8, first_part, 0)
    stage_z(CH - 1)
    w_hand_on(3, last=True)
    w_hand_far(3)

    def drain_chunk(g, unused):
        for n in range(1, 8):
            q_copy(g, n).wait_send()
        for a in range(2):
            m_copy(g, a, 1).wait_send()

            @pl.when(jnp.logical_not(m_is_self(a)))
            def _():
                m_copy(g, a, 0).wait_send()

        return unused

    lax.fori_loop(0, CH, drain_chunk, 0)
    z_wait(CH - 2)
    w_partner(3)

    def second_part(place, unused):
        multiply(0, CH - 2, place, 384, 512)
        multiply(CH - 2, 1, place, 0, 512)
        return unused

    lax.fori_loop(0, 8, second_part, 0)
    for g in range(CH - 1):
        csend[g] = acc[g, 1 - yl].astype(BF16)

    def swap(n):
        some = pl.ds(0, CH - 1) if n == 0 else pl.ds(CH - 1, 1)
        return remote(csend.at[some], cbuf.at[some], c_send.at[n], c_recv.at[n], y_mate)

    swap(0).start()

    def last_part(place, unused):
        multiply(CH - 1, 1, place, 0, 512)
        return unused

    last_part(z, 0)
    last_part(zz(4), 0)
    for n, d in ((4, -1), (5, 1), (0, -2), (1, 2), (2, 3), (3, -3)):
        z_take(CH - 1, n)
        last_part(zz(d), 0)
    csend[CH - 1] = acc[CH - 1, 1 - yl].astype(BF16)
    swap(1).start()
    for copy in kv_out:
        copy.wait_send()
    w_forward(0).wait_send()
    for j in range(4):
        for d in range(1, 4):
            if d == 2 and j < 3:
                w_on(j).wait_send()
            else:
                w_copy(d, j).wait_send()
            w_pass(d, j).wait_send()
    for g in range(CH - 1):
        for copy in z_copies(g):
            copy.wait_send()
    for copy in z_copies(CH - 1):
        copy.wait_send()
    swap(0).wait_recv()
    for g in range(CH):
        if g == CH - 1:
            swap(1).wait_recv()
        out_ref[pl.ds(g * RG, RG), :] = (acc[g, yl] + cbuf[g].astype(F32)).astype(BF16)

    for n in range(2):
        swap(n).wait_send()


def local(queries, cache_keys, cache_values, new_keys, new_values, out_weight):
    dma = pltpu.SemaphoreType.DMA
    hbm = pl.BlockSpec(memory_space=pltpu.HBM)
    vmem = pl.BlockSpec(memory_space=pltpu.VMEM)
    items = 2 * CH
    return pl.pallas_call(
        kernel,
        out_shape=jax.ShapeDtypeStruct((128, 512), BF16),
        in_specs=[vmem, hbm, hbm, hbm, hbm, hbm],
        out_specs=vmem,
        scratch_shapes=[
            pltpu.VMEM((KEYS, HD), BF16),
            pltpu.VMEM((KEYS, HD), BF16),
            pltpu.VMEM((VR, KEYS), BF16),
            pltpu.VMEM((KEYS, COLS), F32),
            pltpu.VMEM((8, 128, 512), BF16),
            pltpu.VMEM((HD, COLS), BF16),
            pltpu.VMEM((items, 4, VR, HD), BF16),
            pltpu.VMEM((CH, 8, VR, HD), BF16),
            pltpu.VMEM((CH, RG, 512), BF16),
            pltpu.VMEM((8, CH, 2, RG, 512), BF16),
            pltpu.VMEM((8, 512, 512), BF16),
            pltpu.VMEM((CH, 2, RG, 512), F32),
            pltpu.VMEM((CH, RG, 512), BF16),
            pltpu.VMEM((CH, RG, 512), BF16),
            dma((8,)), dma((4,)), dma((4,)), dma((CH, 8)), dma((CH, 8)),
            dma((4, 4)), dma((8, 4)), dma((4, 4)),
            dma((items, 4)), dma((CH, 8)),
            dma((CH, 2, 2)), dma((CH, 2, 2)), dma((CH, 6)), dma((CH, 6)),
            dma((2,)), dma((2,)),
        ],
        compiler_params=pltpu.CompilerParams(
            collective_id=0, has_side_effects=True, vmem_limit_bytes=60 * 2**20
        ),
        cost_estimate=pl.CostEstimate(
            flops=11_000_000_000, bytes_accessed=4_000_000, transcendentals=18_000_000
        ),
    )(queries, cache_keys, cache_values, new_keys, new_values, out_weight)


def solution(mesh):
    placed = (
        P("seq", "head"),
        P("seq", None),
        P("seq", None),
        P("seq", None),
        P("seq", None),
        P("seq", "head"),
    )
    return jax.shard_map(
        local, mesh=mesh, in_specs=placed, out_specs=P("seq", "head"), check_vma=False
    )
```
